512 devices in a mesh: sector: 64 (over z, x), chan: 8 (over y, core).
Axes of the slice: x: 4, y: 4, z: 16, core: 2. Of those that a mesh axis runs over, the one named last changes fastest.
Arguments:
- psi: float32 [2, 4096, 4096], P(None, 'chan', 'sector'), may hold values from -6 to 6
- potential: bfloat16 [4096, 4096], P('chan', 'sector'), may hold values from -0.796875 to 0.796875
- dipole: bfloat16 [16, 8, 256, 256], P('chan'), may hold values from -0.125 to 0.125
- coupling: int32 [16, 8], P('chan'), may hold values from 0 to 15
- amp: bfloat16 [4096, 2048], P('chan'), may hold values from -0.125 to 0.125
- sym: int32 [4096], P('chan'), may hold values from 0 to 15
- sizes: int32 [16], P('chan'), may hold values from 1 to 2048, 24576 in all
- inner_ham: bfloat16 [16, 2048, 2048], P('chan', 'sector'), as said below
- inner_state: float32 [2, 16, 2048], P(None, 'chan'), may hold values from -6 to 6
- field: float32 [1], replicated, may hold values from 0.5 to 1.5
Outputs:
- psi_next: float32 [2, 4096, 4096], P(None, 'chan', 'sector')
- state_next: float32 [2, 16, 2048], P(None, 'chan')
The draws below stay inside these ranges and needn't reach their ends.
Inputs may be any that keep to these rules, and one draw needn't show every extreme that they name: `coupling`: block indices. `sym`: symmetry block indices. The sizes sum to 24576. `inner_ham`: each block is symmetric.
All inputs are finite; a program needn't handle non-finite values. No bound on the sum of `sizes` on one device may be relied on, other than what follows from the above.
Results may differ from the reference program's by a relative error of at most 0.002.
The reference program's roundings to bfloat16 on the way (of `low`) count: a program that leaves them out, or rounds other values in their place, can miss the bound.
Values may be sent and summed in bfloat16 or wider, within the bound.
No kernel may reach another device: no remote copies, remote signals or barrier semaphores. Data moves between devices by JAX's collectives and lax.ppermute only.
A program may use at most 64 MiB of HBM per device.

```python
import math
import jax
import jax.numpy as jnp
import numpy as np
from jax import lax

CHANNELS = 4096
CBS = 256
NCOUP = 8
PTS = 64
B = 2048
ORDER = 4
NBLK = 16
NSYM = 16
NR = 4096


def draw_psi(key, part):
    key = jax.random.fold_in(key, 5)
    values = jax.random.truncated_normal(key, -6.0, 6.0, (2, CHANNELS, NR), jnp.float32)
    scale = jnp.where(jnp.arange(NR) < PTS, 0.01, 1.0).astype(jnp.float32)
    return values * scale[None, None, :]


def draw_inner_ham(key, part):
    key = jax.random.fold_in(key, 11)
    values = jax.random.normal(key, (NSYM, B, B), jnp.float32)
    sym_part = (values + jnp.swapaxes(values, 1, 2)) * (0.5 / B ** 0.5)
    return sym_part.astype(jnp.bfloat16)


def with_ends(entries, stream_key, low, largest):
    longest = entries.shape.index(max(entries.shape))
    spots = []
    for shift in (0, 1):
        where = [jax.random.randint(jax.random.fold_in(stream_key, axis), (), 0, length) for axis, length in enumerate(entries.shape)]
        where[longest] = (where[longest] + shift) % entries.shape[longest]
        spots.append(tuple(where))
    return entries.at[spots[0]].set(low).at[spots[1]].set(largest)


def level_of(key, extent, cuts, least, high):
    def one(position, parts):
        heights = jax.random.uniform(jax.random.fold_in(jax.random.fold_in(key, 6), position), (parts,), jnp.float32, least / len(cuts), high / len(cuts))
        return jnp.repeat(jnp.exp(heights), extent[position] // parts).reshape((-1,) + (1,) * (len(extent) - position - 1))

    level = one(*cuts[0])
    for cut in cuts[1:]:
        level = level * one(*cut)
    return level


def profile(amount, total, reach, skew):
    loads = [(1 << 20) // math.isqrt(grade ** skew) + 1 for grade in range(2, amount + 1)]
    rest, holding = total - reach - (amount - 1), [1] * (amount - 1)
    while rest > 0:
        candidates = [i for i in range(amount - 1) if holding[i] < reach]
        mass, left = sum([loads[i] for i in candidates]), rest
        for i in candidates:
            extra = min(reach - holding[i], max(1, left * loads[i] // mass), rest)
            holding[i] = holding[i] + extra
            rest = rest - extra
    return np.array([reach] + holding)


def ragged(rng, amount, total, bound, skew):
    if amount == 2:
        one = jax.random.randint(rng, (), max(1, total - bound), min(bound, total - 1) + 1)
        return jnp.stack([one, total - one])
    tallies = jnp.asarray(profile(amount, total, bound, skew), jnp.int32)
    couples = (amount - 1) // 2
    giver, sink = tallies[1:1 + 2 * couples:2], tallies[2:2 + 2 * couples:2]
    slack = jnp.minimum(giver - 1, bound - sink)
    moved = jax.random.randint(jax.random.fold_in(rng, 1), (couples,), 0, 1 << 20) % (slack + 1)
    tallies = tallies.at[1:1 + 2 * couples:2].set(giver - moved).at[2:2 + 2 * couples:2].set(sink + moved)
    return tallies[jax.random.permutation(jax.random.fold_in(rng, 2), amount)]


def centred(rng, shape, width, bound, cuts=(), held_as=jnp.bfloat16):
    result = width * jax.random.normal(rng, shape, jnp.float32)
    if cuts:
        result = result * level_of(rng, shape, cuts, -0.22, 0.18)
    return jnp.clip(result, -bound, bound).astype(held_as)


def setup_inputs(seed: int = 0) -> dict:
    streams_of = jax.random.split(jax.random.key(seed), 11)
    psi = draw_psi(jax.random.fold_in(streams_of[10], 71), 0)
    potential = jnp.clip(jax.random.uniform(streams_of[1], (CHANNELS, NR), jnp.float32, -0.796875, 0.796875) * level_of(streams_of[1], (CHANNELS, NR), ((0, 8), (1, 64)), -0.4, 0.0), -0.796875, 0.796875).astype(jnp.bfloat16)
    dipole = centred(streams_of[2], (NBLK, NCOUP, CBS, CBS), (NCOUP * CBS) ** -0.5, 0.125, ((0, 8),))
    coupling = with_ends(jax.random.randint(streams_of[3], (NBLK, NCOUP), 0, NBLK), jax.random.fold_in(streams_of[3], 1), 0, NBLK - 1).astype(jnp.int32)
    amp = centred(streams_of[4], (CHANNELS, B), B ** -0.5, 0.125, ((0, 8),))
    sym = with_ends(jax.random.randint(streams_of[5], (CHANNELS,), 0, NSYM), jax.random.fold_in(streams_of[5], 1), 0, NSYM - 1).astype(jnp.int32)
    sizes = ragged(streams_of[6], NSYM, NSYM * 3 * B // 4, B, 1).astype(jnp.int32)
    inner_ham = draw_inner_ham(jax.random.fold_in(streams_of[10], 71), 0)
    inner_state = centred(streams_of[8], (2, NSYM, B), 1.0, 6.0, ((1, 8),), jnp.float32)
    field = jnp.clip(jax.random.uniform(streams_of[9], (1,), jnp.float32, 0.5, 1.5), 0.5, 1.5)
    return dict(psi=psi, potential=potential, dipole=dipole, coupling=coupling, amp=amp, sym=sym, sizes=sizes, inner_ham=inner_ham, inner_state=inner_state, field=field)


kinetic_coeff = 1.0 / 48.0


def reference(psi, potential, dipole, coupling, amp, sym, sizes, inner_ham, inner_state, field):
    hi = lax.Precision.HIGHEST
    nr = psi.shape[2]
    radius = (jnp.arange(nr) + 1).astype(jnp.float32) / nr
    mask = (jnp.arange(B)[None, :] < sizes[:, None]).astype(jnp.float32)
    onehot = (sym[None, :] == jnp.arange(NSYM)[:, None]).astype(jnp.float32)
    amp_f = amp.astype(jnp.float32)
    ham_f = inner_ham.astype(jnp.float32)
    pot = potential.astype(jnp.float32)
    strength = field[0]

    def dipole_part(term):
        low = term.astype(jnp.bfloat16).reshape(2, NBLK, CBS, nr)

        def one_block(pair):
            block, index = pair
            picked = low[:, index].astype(jnp.float32)
            return jnp.einsum('jci,zjip->zcp', block.astype(jnp.float32), picked, precision=hi)

        out = lax.map(one_block, (dipole, coupling))
        return jnp.transpose(out, (1, 0, 2, 3)).reshape(2, CHANNELS, nr)

    def apply(term, state):
        product = jnp.einsum('zsk,ck->zsc', state, amp_f, precision=hi)
        ghost = jnp.sum(product * onehot[None], axis=1)
        left = jnp.broadcast_to(ghost[:, :, None], (2, CHANNELS, 2))
        padded = jnp.concatenate([left, term, jnp.zeros((2, CHANNELS, 2), jnp.float32)], axis=2)
        stencil = -padded[:, :, :-4] + 16.0 * padded[:, :, 1:-3] - 30.0 * term + 16.0 * padded[:, :, 3:-1] - padded[:, :, 4:]
        outer = -kinetic_coeff * stencil + pot * term + strength * radius * dipole_part(term)
        chosen = onehot[None] * term[:, :, 0][:, None, :]
        surface = jnp.einsum('zsc,ck->zsk', chosen, amp_f, precision=hi)
        inner = mask * (jnp.einsum('skl,zsl->zsk', ham_f, state, precision=hi) + surface)
        return outer, inner

    term = psi
    state = mask * inner_state
    total = term
    total_in = state
    for order in range(1, ORDER + 1):
        outer, inner = apply(term, state)
        term = jnp.stack([outer[1], -outer[0]]) / order
        state = jnp.stack([inner[1], -inner[0]]) / order
        total = total + term
        total_in = total_in + state
    return total, total_in
```

```python
from types import SimpleNamespace

import jax
import jax.numpy as jnp
from jax import lax
from jax.experimental import pallas as pl
from jax.experimental.pallas import tpu as pltpu
from jax.sharding import PartitionSpec as P


F32 = jnp.float32
BF16 = jnp.bfloat16
VMEM = pltpu.VMEM
SMEM = pltpu.SMEM
KINETIC = 1.0 / 48.0


def call(body, ins, outs, scratch, flops, moved):
    names = list(ins) + list(outs) + list(scratch)

    def kernel(*refs):
        body(SimpleNamespace(**dict(zip(names, refs))))

    results = pl.pallas_call(
        kernel,
        out_shape=[jax.ShapeDtypeStruct(shape, kind) for shape, kind in outs.values()],
        in_specs=[pl.BlockSpec(memory_space=space) for _, space in ins.values()],
        out_specs=[pl.BlockSpec(memory_space=VMEM) for _ in outs],
        scratch_shapes=list(scratch.values()),
        compiler_params=pltpu.CompilerParams(vmem_limit_bytes=24 * 1024 * 1024),
        cost_estimate=pl.CostEstimate(flops=flops, bytes_accessed=moved, transcendentals=0),
    )(*[value for value, _ in ins.values()])
    return dict(zip(outs, results))


def dot_t(a, b):
    return lax.dot_general(a, b, (((1,), (1,)), ((), ())), preferred_element_type=F32)


def dot(a, b):
    return lax.dot_general(a, b, (((1,), (0,)), ((), ())), preferred_element_type=F32)


def split(value):
    high = value.astype(BF16)
    return high, (value - high.astype(F32)).astype(BF16)


def rows_of(shape):
    return lax.broadcasted_iota(jnp.int32, shape, 0)


def fetch(r):
    mine = r.info[0]
    copies = [
        pltpu.make_async_copy(r.ya, r.ys.at[mine], r.sem.at[0]),
        pltpu.make_async_copy(r.yb, r.ys.at[1 - mine], r.sem.at[1]),
    ]
    for copy in copies:
        copy.start()
    return copies


def ghost_of(r, base):
    states = jnp.concatenate([r.ys[c, y, base : base + 16, :] for y in range(4) for c in range(2)], axis=0)
    row = rows_of((128, 512))
    quarter = (row >> 1) & 3
    total = jnp.zeros((128, 512), F32)
    for q in range(4):
        part = dot_t(states, r.amp[:, q * 512 : (q + 1) * 512])
        total = total + jnp.where(quarter == q, part, 0.0)
    block = (row >> 4) * 2 + (row & 1)
    total = jnp.where(block == r.sym[...], total, 0.0)
    comp = (row >> 3) & 1
    g0 = jnp.sum(jnp.where(comp == 0, total, 0.0), axis=0, keepdims=True)
    g1 = jnp.sum(jnp.where(comp == 1, total, 0.0), axis=0, keepdims=True)
    return g0, g1


def surface_part(r, first0, first1):
    row = rows_of((128, 512))
    block = (row >> 4) * 2 + (row & 1)
    comp = (row >> 3) & 1
    chosen = jnp.where(block == r.sym[...], jnp.where(comp == 0, first0, first1), 0.0)
    both = jnp.concatenate(split(chosen), axis=0)
    quarter = (row >> 1) & 3
    total = jnp.zeros((128, 512), F32)
    for q in range(4):
        part = dot(both, r.amp[:, q * 512 : (q + 1) * 512])
        total = total + jnp.where(quarter == q, part[:128] + part[128:], 0.0)
    return total.astype(BF16)


def surface_of(r, base):
    mine = r.info[0]
    total = jnp.zeros((16, 512), F32)
    for y in range(4):
        for c in range(2):
            both = r.ys[c, y, base : base + 32, :].astype(F32)
            total = total + jnp.where(mine == 0, both[:16], both[16:])
    return total


def mask_of(r):
    row = rows_of((16, 512))
    lane = lax.broadcasted_iota(jnp.int32, (16, 512), 1)
    size = jnp.where((row & 1) == 0, r.sizes[0], r.sizes[1])
    return (((row >> 1) & 3) * 512 + lane) < size


def ham_full(r):
    for z in range(16):
        for comp in range(2):
            at = comp * 8 + (z // 4) * 2
            r.full[at : at + 2, (z % 4) * 128 : (z % 4 + 1) * 128] = r.zr[z, comp * 2 : comp * 2 + 2, :]
    return r.full[...]


def next_state(r, ham, surface, order):
    image = jnp.where(mask_of(r), ham + surface, 0.0)
    return jnp.concatenate([image[8:], -image[:8]], axis=0) * (1.0 / order)


def first_received(r):
    for comp in range(2):
        for part in range(4):
            at = 8 + comp * 4 + part
            r.first[comp : comp + 1, part * 128 : (part + 1) * 128] = r.zr[0, at : at + 1, :]
    return r.first[0:1, :], r.first[1:2, :]


def ham_rows(r, state):
    both = jnp.concatenate(split(state), axis=0)
    row = rows_of((16, 128))
    total = jnp.zeros((16, 128), F32)
    for block in range(2):
        for q in range(4):
            ham = jnp.concatenate([r.ham[x, block, :, q * 512 : (q + 1) * 512] for x in range(4)], axis=0)
            part = dot_t(both, ham)
            keep = (((row >> 1) & 3) == q) & ((row & 1) == block)
            total = total + jnp.where(keep, part[:16] + part[16:], 0.0)
    r.sums[...] = total
    for comp in range(2):
        at = comp * 8
        r.piece[comp * 2 : comp * 2 + 2, :] = (
            r.sums[at : at + 2, :] + r.sums[at + 2 : at + 4, :] + r.sums[at + 4 : at + 6, :] + r.sums[at + 6 : at + 8, :]
        )


def first_rows(r, first0, first1):
    for comp, first in enumerate((first0, first1)):
        for part in range(4):
            at = 8 + comp * 4 + part
            r.piece[at : at + 1, :] = first[:, part * 128 : (part + 1) * 128]


def z_out(r):
    piece = r.piece[...]
    for z in range(16):
        r.zo[z] = piece


def dipole_image(r):
    halves = []
    for b in range(2):
        total = None
        for j in range(8):
            n = r.coupling[b, j]
            lanes = pl.ds(pl.multiple_of((n & 1) * 256, 256), 256)
            block = r.ys[(n >> 1) & 1, n >> 2, 0:128, lanes]
            part = dot_t(block, r.dipole[b, j])
            total = part if total is None else total + part
        halves.append(total)
    return jnp.concatenate(halves, axis=1)


def outer_image(r, dip):
    images = []
    row = rows_of((64, 512))
    radius = (r.info[1] * 64 + row + 1).astype(F32) * (1.0 / r.points)
    for comp in range(2):
        u = r.u[comp * 64 : (comp + 1) * 64, :]
        r.pad[comp, 6:8, :] = r.left[comp * 2 : comp * 2 + 2, :]
        r.pad[comp, 8:72, :] = u
        r.pad[comp, 72:74, :] = r.right[comp * 2 : comp * 2 + 2, :]
        stencil = 16.0 * (r.pad[comp, 7:71, :] + r.pad[comp, 9:73, :]) - 30.0 * u
        stencil = stencil - (r.pad[comp, 6:70, :] + r.pad[comp, 10:74, :])
        images.append(
            -KINETIC * stencil + r.pot[...] * u + r.field[0] * radius * dip[comp * 64 : (comp + 1) * 64, :]
        )
    return images


def ghost_image(r, ghosts):
    row = rows_of((64, 512))
    hub = jnp.where(r.info[1] == 0, 1.0, 0.0).astype(F32)
    images = []
    for ghost in ghosts:
        ghost = ghost * hub
        images.append(jnp.where(row == 0, (-15.0 * KINETIC) * ghost, jnp.where(row == 1, KINETIC * ghost, 0.0)))
    return images


def term_of(images, order):
    return images[1] * (1.0 / order), images[0] * (-1.0 / order)


def ends_out(r, term):
    for comp in range(2):
        r.head[comp * 2 : comp * 2 + 2, :] = term[comp][0:2, :]
        r.tail[comp * 2 : comp * 2 + 2, :] = term[comp][62:64, :]
    r.head[4:8, :] = jnp.zeros((4, 512), F32)
    r.tail[4:8, :] = jnp.zeros((4, 512), F32)


def low_out(r, term):
    low = jnp.concatenate([term[0].astype(BF16), term[1].astype(BF16)], axis=0)
    for y in range(4):
        r.yo[y, 0:128, :] = low


def state_out(r, state, base):
    low = state.astype(BF16)
    for y in range(4):
        r.yo[y, base : base + 16, :] = low


def surface_out(r, part, base):
    for y in range(4):
        r.yo[y, base : base + 32, :] = part[y * 32 : (y + 1) * 32]


def shards(psi, potential, dipole, coupling, amp, sym, sizes, inner_ham, inner_state, field):
    n_sector = lax.axis_size("sector")
    sector = lax.axis_index("sector")
    chan = lax.axis_index("chan")
    points = float(64 * n_sector)
    x_groups = [[z * 4 + x for x in range(4)] for z in range(16)]
    z_groups = [[z * 4 + x for z in range(16)] for x in range(4)]
    y_groups = [[y * 2 + c for y in range(4)] for c in range(2)]
    swap = [(c, c ^ 1) for c in range(8)]
    up = [(i, i + 1) for i in range(n_sector - 1)]
    down = [(i + 1, i) for i in range(n_sector - 1)]

    info = jnp.stack([chan & 1, sector]).astype(jnp.int32)
    sym_row = sym.reshape(1, 512)
    first_state = inner_state.reshape(2, 2, 4, 512).transpose(0, 2, 1, 3).reshape(16, 512)

    def over_y(piece):
        mine = lax.all_to_all(piece, "chan", 0, 0, axis_index_groups=y_groups)
        return mine, lax.ppermute(mine, "chan", swap)

    def over_z(piece):
        return lax.all_to_all(piece, "sector", 0, 0, axis_index_groups=z_groups)

    def over_x(piece):
        return lax.all_to_all(piece, "sector", 0, 0, axis_index_groups=x_groups)

    def halos(out):
        return lax.ppermute(out["tail"], "sector", up), lax.ppermute(out["head"], "sector", down)

    def stage(body, ins, outs, rows=0, low=False, inner=True):
        ins = dict(ins)
        ins["info"] = (info, SMEM)
        scratch = {"sem": pltpu.SemaphoreType.DMA((2,))}
        moved = 1 << 20
        if rows:
            scratch["ys"] = VMEM((2, 4, rows, 512), BF16)
        if low:
            ins["dipole"] = (dipole, VMEM)
            ins["coupling"] = (coupling, SMEM)
            ins["field"] = (field, SMEM)
            ins["pot"] = (pot, VMEM)
            scratch["pad"] = VMEM((2, 80, 512), F32)
            moved += 3 << 20
        if inner:
            ins["sizes"] = (sizes, SMEM)
            ins["sym"] = (sym_row, VMEM)
            ins["amp"] = (amp, VMEM)
            scratch["full"] = VMEM((16, 512), F32)
            scratch["first"] = VMEM((2, 512), F32)
            scratch["sums"] = VMEM((16, 128), F32)
            scratch["piece"] = VMEM((16, 128), F32)
            moved += 3 << 20

        def whole(r):
            r.points = points
            if "zo" in outs:
                r.piece[...] = jnp.zeros((16, 128), F32)
            body(r)

        return call(whole, ins, outs, scratch, 400_000_000, moved)

    def y_spec(rows):
        return ((4, rows, 512), BF16)

    z_spec = ((16, 16, 128), F32)
    outer_spec = ((128, 512), F32)
    inner_spec = ((16, 512), F32)
    end_spec = ((8, 512), F32)


    def begin(r):
        first = []
        term = []
        for comp in range(2):
            u = r.psi[comp].T
            r.u[comp * 64 : (comp + 1) * 64, :] = u
            term.append(u)
            first.append(u[0:1, :])
        r.pot_o[...] = r.potential[...].astype(F32).T
        low_out(r, term)
        ends_out(r, term)
        state = jnp.where(mask_of(r), r.given[...], 0.0)
        r.state[...] = state
        state_out(r, state, 128)
        first_rows(r, first[0], first[1])
        z_out(r)

    hams = over_x(jnp.broadcast_to(inner_ham[None], (4,) + inner_ham.shape))
    out = stage(
        begin,
        {"psi": (psi, VMEM), "potential": (potential, VMEM), "given": (first_state, VMEM)},
        {"u": outer_spec, "pot_o": ((64, 512), F32), "yo": y_spec(144), "head": end_spec, "tail": end_spec,
         "state": inner_spec, "zo": z_spec},
    )
    pot = out["pot_o"]
    u0, state0 = out["u"], out["state"]
    ya, yb = over_y(out["yo"])
    zr = over_z(out["zo"])
    left, right = halos(out)


    def end0(r):
        copies = fetch(r)
        ham_rows(r, r.state[...])
        part = surface_part(r, *first_received(r))
        surface_out(r, part, 128)
        for copy in copies:
            copy.wait()
        images = outer_image(r, dipole_image(r))
        more = ghost_image(r, ghost_of(r, 128))
        term = term_of([a + b for a, b in zip(images, more)], 1)
        for comp in range(2):
            r.u_o[comp * 64 : (comp + 1) * 64, :] = term[comp]
        first_rows(r, term[0][0:1, :], term[1][0:1, :])
        z_out(r)
        low_out(r, term)
        ends_out(r, term)

    out = stage(
        end0,
        {"ya": (ya, pl.ANY), "yb": (yb, pl.ANY), "zr": (zr, VMEM), "u": (u0, VMEM), "left": (left, VMEM),
         "right": (right, VMEM), "state": (state0, VMEM), "ham": (hams, VMEM)},
        {"u_o": outer_spec, "yo": y_spec(160), "zo": z_spec, "head": end_spec, "tail": end_spec},
        rows=144, low=True,
    )
    u1 = out["u_o"]
    ya, yb = over_y(out["yo"])
    zr = over_z(out["zo"])
    left, right = halos(out)


    def end1(r):
        copies = fetch(r)
        part = surface_part(r, *first_received(r))
        surface_out(r, part, 16)
        ham = ham_full(r)
        for copy in copies:
            copy.wait()
        state = next_state(r, ham, surface_of(r, 128), 1)
        r.state_o[...] = state
        state_out(r, state, 0)
        ham_rows(r, state)
        z_out(r)

    def outer1(r):
        copies = fetch(r)
        for copy in copies:
            copy.wait()
        term = term_of(outer_image(r, dipole_image(r)), 2)
        for comp in range(2):
            r.u_o[comp * 64 : (comp + 1) * 64, :] = term[comp]

    y_in = {"ya": (ya, pl.ANY), "yb": (yb, pl.ANY)}
    out = stage(
        end1,
        {**y_in, "zr": (zr, VMEM), "ham": (hams, VMEM)},
        {"yo": y_spec(48), "zo": z_spec, "state_o": inner_spec},
        rows=160,
    )
    state1 = out["state_o"]
    ya, yb = over_y(out["yo"])
    zr = over_z(out["zo"])
    base2 = stage(
        outer1,
        {**y_in, "u": (u1, VMEM), "left": (left, VMEM), "right": (right, VMEM)},
        {"u_o": outer_spec},
        rows=160, low=True, inner=False,
    )["u_o"]


    def end2(r):
        copies = fetch(r)
        ham = ham_full(r)
        for copy in copies:
            copy.wait()
        state = next_state(r, ham, surface_of(r, 16), 2)
        r.state_o[...] = state
        state_out(r, state, 128)
        more = term_of(ghost_image(r, ghost_of(r, 0)), 2)
        term = [r.u[comp * 64 : (comp + 1) * 64, :] + more[comp] for comp in range(2)]
        for comp in range(2):
            r.u_o[comp * 64 : (comp + 1) * 64, :] = term[comp]
        first = (term[0][0:1, :], term[1][0:1, :])
        first_rows(r, *first)
        ham_rows(r, state)
        z_out(r)
        low_out(r, term)
        ends_out(r, term)
        surface_out(r, surface_part(r, *first), 144)

    out = stage(
        end2,
        {"ya": (ya, pl.ANY), "yb": (yb, pl.ANY), "zr": (zr, VMEM), "u": (base2, VMEM), "ham": (hams, VMEM)},
        {"u_o": outer_spec, "yo": y_spec(176), "zo": z_spec, "head": end_spec, "tail": end_spec, "state_o": inner_spec},
        rows=48,
    )
    u2, state2 = out["u_o"], out["state_o"]
    ya, yb = over_y(out["yo"])
    zr = over_z(out["zo"])
    left, right = halos(out)


    def end3(r):
        copies = fetch(r)
        ham = ham_full(r)
        r.ham_o[...] = ham
        part = surface_part(r, *first_received(r))
        surface_out(r, part, 144)
        for copy in copies:
            copy.wait()
        state_out(r, next_state(r, ham, surface_of(r, 144), 3), 128)
        images = outer_image(r, dipole_image(r))
        more = ghost_image(r, ghost_of(r, 128))
        term = term_of([a + b for a, b in zip(images, more)], 3)
        for comp in range(2):
            r.u_o[comp * 64 : (comp + 1) * 64, :] = term[comp]
        first_rows(r, term[0][0:1, :], term[1][0:1, :])
        z_out(r)
        low_out(r, term)
        ends_out(r, term)

    out = stage(
        end3,
        {"ya": (ya, pl.ANY), "yb": (yb, pl.ANY), "zr": (zr, VMEM), "u": (u2, VMEM), "left": (left, VMEM),
         "right": (right, VMEM)},
        {"u_o": outer_spec, "yo": y_spec(176), "zo": z_spec, "head": end_spec, "tail": end_spec, "ham_o": inner_spec},
        rows=176, low=True,
    )
    u3, image2 = out["u_o"], out["ham_o"]
    ya, yb = over_y(out["yo"])
    zr = over_z(out["zo"])
    left, right = halos(out)


    def end4(r):
        copies = fetch(r)
        surface_out(r, surface_part(r, *first_received(r)), 0)
        for copy in copies:
            copy.wait()
        state = next_state(r, r.image[...], surface_of(r, 144), 3)
        r.state_o[...] = state
        ham_rows(r, state)
        z_out(r)

    def outer4(r):
        copies = fetch(r)
        for copy in copies:
            copy.wait()
        images = outer_image(r, dipole_image(r))
        more = ghost_image(r, ghost_of(r, 128))
        term = term_of([a + b for a, b in zip(images, more)], 4)
        for comp in range(2):
            at = slice(comp * 64, (comp + 1) * 64)
            total = r.u0[at, :] + r.u1[at, :] + r.u2[at, :] + r.u[at, :] + term[comp]
            r.psi_o[comp] = total.T

    y_in = {"ya": (ya, pl.ANY), "yb": (yb, pl.ANY)}
    out = stage(
        end4,
        {**y_in, "zr": (zr, VMEM), "image": (image2, VMEM), "ham": (hams, VMEM)},
        {"yo": y_spec(32), "zo": z_spec, "state_o": inner_spec},
        rows=176,
    )
    state3 = out["state_o"]
    ya, yb = over_y(out["yo"])
    zr = over_z(out["zo"])
    psi_next = stage(
        outer4,
        {**y_in, "u": (u3, VMEM), "u0": (u0, VMEM), "u1": (u1, VMEM), "u2": (u2, VMEM), "left": (left, VMEM),
         "right": (right, VMEM)},
        {"psi_o": ((2, 512, 64), F32)},
        rows=176, low=True,
    )["psi_o"]


    def end5(r):
        copies = fetch(r)
        ham = ham_full(r)
        for copy in copies:
            copy.wait()
        state = next_state(r, ham, surface_of(r, 0), 4)
        total = r.s0[...] + r.s1[...] + r.s2[...] + r.s3[...] + state
        for x in range(4):
            r.sum_o[x] = total

    total = stage(
        end5,
        {"ya": (ya, pl.ANY), "yb": (yb, pl.ANY), "zr": (zr, VMEM), "s0": (state0, VMEM), "s1": (state1, VMEM),
         "s2": (state2, VMEM), "s3": (state3, VMEM)},
        {"sum_o": ((4, 16, 512), F32)},
        rows=32,
    )["sum_o"]
    state_next = over_x(total)[0].reshape(2, 4, 2, 512).transpose(0, 2, 1, 3).reshape(2, 2, 2048)
    return psi_next, state_next


def solution(mesh):
    return jax.shard_map(
        shards,
        mesh=mesh,
        in_specs=(
            P(None, "chan", "sector"),
            P("chan", "sector"),
            P("chan", None, None, None),
            P("chan", None),
            P("chan", None),
            P("chan"),
            P("chan"),
            P("chan", "sector", None),
            P(None, "chan", None),
            P(),
        ),
        out_specs=(P(None, "chan", "sector"), P(None, "chan", None)),
        check_vma=False,
    )
```

```python
import itertools
from types import SimpleNamespace

import jax
import jax.numpy as jnp
from jax import lax
from jax.experimental import pallas as pl
from jax.experimental.pallas import tpu as pltpu
from jax.sharding import PartitionSpec as P


F32 = jnp.float32
BF16 = jnp.bfloat16
VMEM = pltpu.VMEM
SMEM = pltpu.SMEM
KINETIC = 1.0 / 48.0


KEPT = ("u", "state", "amp", "dipole", "ham", "mark")
BIG = ("keep_amp", "keep_dipole", "keep_ham", "ys")


def call(body, ins, outs, scratch, flops):
    arrays = dict(ins)
    scratch = dict(scratch)
    for name, value in arrays.items():
        if name not in ("info", "field") + KEPT and not name.startswith("keep_"):
            scratch[name + "_v"] = VMEM(value.shape, value.dtype)
    scratch["info_s"] = SMEM((128,), jnp.int32)
    scratch["field_s"] = SMEM((128,), F32)
    parts = {name: 4 if name in BIG else 1 for name in arrays if name not in KEPT}
    first_sem = dict(zip(parts, itertools.accumulate([0] + list(parts.values()))))
    scratch["sem"] = pltpu.SemaphoreType.DMA((sum(parts.values()),))
    names = [name if name in KEPT else "hbm_" + name for name in arrays] + list(outs) + list(scratch)

    def kernel(*refs):
        r = SimpleNamespace(**dict(zip(names, refs)))
        copies = {}

        def target(name):
            if name.startswith("keep_"):
                return getattr(r, name[5:] + "_o")
            return getattr(r, name + ("_s" if name in ("info", "field") else "_v"))

        def start(name):
            source, dest = getattr(r, "hbm_" + name), target(name)
            views = [(source, dest)]
            if name == "keep_dipole":
                views = [(source.at[b, pl.ds(j, 4)], dest.at[b, pl.ds(j, 4)]) for b in range(2) for j in (0, 4)]
            elif name in BIG:
                size = source.shape[0] // 4
                views = [(source.at[pl.ds(i * size, size)], dest.at[pl.ds(i * size, size)]) for i in range(4)]
            copies[name] = [
                pltpu.make_async_copy(view[0], view[1], r.sem.at[first_sem[name] + i]) for i, view in enumerate(views)
            ]
            for copy in copies[name]:
                copy.start()

        def wait(*wanted):
            for name in wanted:
                if name in copies:
                    for copy in copies.pop(name):
                        copy.wait()
                    setattr(r, name, target(name))

        r.wait = wait
        for name in arrays:
            if name not in KEPT:
                start(name)
        wait("info")
        body(r)
        wait(*list(copies))

    results = pl.pallas_call(
        kernel,
        out_shape=[jax.ShapeDtypeStruct(shape, kind) for shape, kind in outs.values()],
        in_specs=[pl.BlockSpec(memory_space=VMEM if name in KEPT else pltpu.HBM) for name in arrays],
        out_specs=[pl.BlockSpec(memory_space=VMEM) for _ in outs],
        scratch_shapes=list(scratch.values()),
        compiler_params=pltpu.CompilerParams(vmem_limit_bytes=52 * 1024 * 1024),
        cost_estimate=pl.CostEstimate(flops=flops, bytes_accessed=1024, transcendentals=0),
    )(*arrays.values())
    return dict(zip(outs, results))


def dot_t(a, b):
    return lax.dot_general(a, b, (((1,), (1,)), ((), ())), preferred_element_type=F32)


def dot(a, b):
    return lax.dot_general(a, b, (((1,), (0,)), ((), ())), preferred_element_type=F32)


def split(value):
    high = value.astype(BF16)
    return high, (value - high.astype(F32)).astype(BF16)


def rows_of(shape):
    return lax.broadcasted_iota(jnp.int32, shape, 0)


def ghost_of(r):
    states = jnp.concatenate([r.pr[c, 16:32, :] for c in range(8)], axis=0)
    row = rows_of((128, 512))
    quarter = (row >> 1) & 3
    total = jnp.zeros((128, 512), F32)
    for q in range(4):
        part = dot_t(states, r.amp[:, q * 512 : (q + 1) * 512])
        total = total + jnp.where(quarter == q, part, 0.0)
    block = (row >> 4) * 2 + (row & 1)
    total = jnp.where(block == r.sym[...], total, 0.0)
    comp = (row >> 3) & 1
    g0 = jnp.sum(jnp.where(comp == 0, total, 0.0), axis=0, keepdims=True)
    g1 = jnp.sum(jnp.where(comp == 1, total, 0.0), axis=0, keepdims=True)
    return g0, g1


def surface_part(r, first0, first1):
    row = rows_of((32, 512))
    block = (row >> 2) * 2 + (row & 1)
    chosen = jnp.where(block == r.sym[...], jnp.where(((row >> 1) & 1) == 0, first0, first1), 0.0)
    both = jnp.concatenate(split(chosen), axis=0)
    for q in range(4):
        part = dot(both, r.amp[:, q * 512 : (q + 1) * 512])
        r.sum[...] = part[:32] + part[32:]
        for c in range(8):
            for comp in range(2):
                at = c * 16 + comp * 8 + q * 2
                r.terms[at : at + 2, :] = r.sum[c * 4 + comp * 2 : c * 4 + comp * 2 + 2, :]


def surface_of(r):
    total = r.pr[0, 0:16, :].astype(F32)
    for c in range(1, 8):
        total = total + r.pr[c, 0:16, :].astype(F32)
    return total


def mask_of(r):
    row = rows_of((16, 512))
    lane = lax.broadcasted_iota(jnp.int32, (16, 512), 1)
    size = jnp.where((row & 1) == 0, r.info[16], r.info[17])
    return (((row >> 1) & 3) * 512 + lane) < size


def ham_full(r):
    for z in range(16):
        for comp in range(2):
            at = comp * 8 + (z // 4) * 2
            for block in range(2):
                lanes = (comp * 2 + block) * 128
                r.full[at + block : at + block + 1, (z % 4) * 128 : (z % 4 + 1) * 128] = r.zr[z, :, lanes : lanes + 128]
    return r.full[...]


def next_state(r, ham, surface, order):
    image = jnp.where(mask_of(r), ham + surface, 0.0)
    return jnp.concatenate([image[8:], -image[:8]], axis=0) * (1.0 / order)


def first_received(r):
    return r.zr[0, :, 512:1024], r.zr[0, :, 1024:1536]


def ham_rows(r, state):
    both = jnp.concatenate(split(state), axis=0)
    row = rows_of((16, 128))
    total = jnp.zeros((16, 128), F32)
    for block in range(2):
        for q in range(4):
            ham = jnp.concatenate([r.ham[x, block, :, q * 512 : (q + 1) * 512] for x in range(4)], axis=0)
            part = dot_t(both, ham)
            keep = (((row >> 1) & 3) == q) & ((row & 1) == block)
            total = total + jnp.where(keep, part[:16] + part[16:], 0.0)
    r.sums[...] = total
    for comp in range(2):
        for block in range(2):
            at = comp * 8 + block
            rows = [r.sums[at + 2 * q : at + 2 * q + 1, :] for q in range(4)]
            lanes = (comp * 2 + block) * 128
            r.piece[:, lanes : lanes + 128] = (rows[0] + rows[1]) + (rows[2] + rows[3])


def first_out(r, first0, first1):
    r.piece[:, 512:1024] = first0
    r.piece[:, 1024:1536] = first1


def z_out(r):
    piece = r.piece[...]
    for z in range(16):
        r.zo[z] = piece


def dipole_image(r):
    for b in range(2):
        total = None
        for j in range(8):
            n = r.info[b * 8 + j]
            lanes = pl.ds(pl.multiple_of((n & 1) * 256, 256), 256)
            part = dot_t(r.ys[n >> 1, 0:160, lanes], r.dipole[b, j])
            total = part if total is None else total + part
        r.dip[:, b * 256 : (b + 1) * 256] = total


def outer_term(r, order):
    images = []
    row = rows_of((80, 512))
    point = r.info[18] * 64 + row - 8
    radius = (point + 1).astype(F32) * (1.0 / r.points)
    for comp in range(2):
        u = r.u[comp * 80 : (comp + 1) * 80, :]
        r.pad[comp, 0:8, :] = jnp.zeros((8, 512), F32)
        r.pad[comp, 8:88, :] = u
        r.pad[comp, 88:96, :] = jnp.zeros((8, 512), F32)
        stencil = 16.0 * (r.pad[comp, 7:87, :] + r.pad[comp, 9:89, :]) - 30.0 * u
        stencil = stencil - (r.pad[comp, 6:86, :] + r.pad[comp, 10:90, :])
        image = -KINETIC * stencil + r.pot[...] * u + r.field[0] * radius * r.dip[comp * 80 : (comp + 1) * 80, :]
        images.append(jnp.where((point >= 0) & (point < r.all_points), image, 0.0))
    return images[1] * (1.0 / order), images[0] * (-1.0 / order)


def ghost_term(r, order):
    row = rows_of((8, 512))
    hub = jnp.where(r.info[18] == 0, 1.0 / order, 0.0).astype(F32)
    images = []
    for ghost in ghost_of(r):
        ghost = ghost * hub
        images.append(jnp.where(row == 0, (-15.0 * KINETIC) * ghost, jnp.where(row == 1, KINETIC * ghost, 0.0)))
    return images[1], -images[0]


def shards(psi, potential, dipole, coupling, amp, sym, sizes, inner_ham, inner_state, field):
    n_sector = lax.axis_size("sector")
    sector = lax.axis_index("sector")
    all_points = 64 * n_sector
    x_groups = [[z * 4 + x for x in range(4)] for z in range(16)]
    z_groups = [[z * 4 + x for z in range(16)] for x in range(4)]
    up = [(i, i + 1) for i in range(n_sector - 1)]
    down = [(i + 1, i) for i in range(n_sector - 1)]

    info = jnp.concatenate([coupling.reshape(16), sizes, sector[None].astype(jnp.int32), jnp.zeros((109,), jnp.int32)])
    common = {"info": info, "sym": sym.reshape(1, 512)}
    strength = jnp.broadcast_to(field, (128,))

    def over_z(piece):
        return lax.all_to_all(piece, "sector", 0, 0, axis_index_groups=z_groups)

    def over_x(piece):
        return lax.all_to_all(piece, "sector", 0, 0, axis_index_groups=x_groups)

    low_spec = ((160, 512), BF16)
    z_spec = ((16, 1, 1536), F32)
    outer_spec = ((160, 512), F32)
    inner_spec = ((16, 512), F32)
    end_spec = ((24, 512), F32)
    z_scratch = {"sums": VMEM((16, 128), F32), "piece": VMEM((1, 1536), F32)}
    surface_scratch = {"sum": VMEM((32, 512), F32), "terms": VMEM((128, 512), F32)}
    full_scratch = {"full": VMEM((16, 512), F32)}
    outer_scratch = {"dip": VMEM((160, 512), F32), "pad": VMEM((2, 96, 512), F32)}


    def prepare(r):
        r.wait("ham", "psi", "pot")
        for x in range(4):
            r.copies[x] = r.ham[...]
        for comp in range(2):
            r.head[comp * 8 : (comp + 1) * 8, :] = r.psi[comp, 0:8, :]
            r.tail[comp * 8 : (comp + 1) * 8, :] = r.psi[comp, 56:64, :]
        r.head[16:24, :] = r.pot[0:8, :].astype(F32)
        r.tail[16:24, :] = r.pot[56:64, :].astype(F32)

    own = {"psi": psi.transpose(0, 2, 1), "pot": potential.T}
    out = call(
        prepare,
        {"info": info, "ham": inner_ham, **own},
        {"copies": ((4,) + inner_ham.shape, BF16), "head": end_spec, "tail": end_spec},
        {}, 1_000_000,
    )
    hams = over_x(out["copies"])
    out_kept = call(
        lambda r: None, {"keep_amp": amp, "keep_dipole": dipole},
        {"amp_o": (amp.shape, BF16), "dipole_o": (dipole.shape, BF16)}, {}, 1_000_000,
    )
    amp, dipole = out_kept["amp_o"], out_kept["dipole_o"]
    left = lax.ppermute(out["tail"], "sector", up)
    right = lax.ppermute(out["head"], "sector", down)

    def begin(r):
        r.wait("psi", "pot", "left", "right", "given")
        for comp in range(2):
            for q in range(4):
                at = comp * 8 + q * 2
                r.state_o[at : at + 2, :] = r.given[comp, :, q * 512 : (q + 1) * 512]
            at = comp * 80
            r.u_o[at : at + 8, :] = r.left[comp * 8 : (comp + 1) * 8, :]
            r.u_o[at + 8 : at + 72, :] = r.psi[comp]
            r.u_o[at + 72 : at + 80, :] = r.right[comp * 8 : (comp + 1) * 8, :]
        r.pot_o[0:8, :] = r.left[16:24, :]
        r.pot_o[8:72, :] = r.pot[...].astype(F32)
        r.pot_o[72:80, :] = r.right[16:24, :]
        r.low_o[...] = r.u_o[...].astype(BF16)
        state = jnp.where(mask_of(r), r.state_o[...], 0.0)
        r.state_o[...] = state
        first_out(r, r.u_o[8:9, :], r.u_o[88:89, :])
        r.wait("keep_ham")
        r.ham = r.ham_o
        ham_rows(r, state)
        z_out(r)

    out = call(
        begin,
        {"info": info, **own, "left": left, "right": right, "given": inner_state, "keep_ham": hams},
        {"ham_o": (hams.shape, BF16), "u_o": outer_spec, "pot_o": ((80, 512), F32), "state_o": inner_spec, "low_o": low_spec, "zo": z_spec},
        z_scratch, 1_000_000_000,
    )
    outer = [out["u_o"]]
    inner = [out["state_o"]]
    pot = out["pot_o"]
    hams = out["ham_o"]


    def surface_body(r):
        for c in range(8):
            r.po[c, 16:32, :] = r.state[...].astype(BF16)
        r.wait("zr", "sym", "amp")
        surface_part(r, *first_received(r))
        for c in range(8):
            r.po[c, 0:16, :] = r.terms[c * 16 : (c + 1) * 16, :].astype(BF16)

    def outer_body(order):
        def body(r):
            r.points = float(all_points)
            r.all_points = all_points
            r.wait("pr", "sym")
            more = ghost_term(r, order)
            r.wait("ys", "field", "pot")
            dipole_image(r)
            term = outer_term(r, order)
            for comp in range(2):
                at = comp * 80
                head = term[comp][8:16, :] + more[comp]
                if order == 4:
                    r.wait("u0", "u1", "u2")
                    total = r.u[at + 8 : at + 72, :] + r.u0[at + 8 : at + 72, :] + r.u1[at + 8 : at + 72, :] + r.u2[at + 8 : at + 72, :]
                    r.psi_o[comp] = total + term[comp][8:72, :]
                    r.psi_o[comp, 0:8, :] = total[0:8, :] + head
                    r.mark_o[comp] = head[:, 0:128]
                else:
                    r.u_o[at : at + 80, :] = term[comp]
                    r.u_o[at + 8 : at + 16, :] = head
            if order < 4:
                r.low_o[...] = r.u_o[...].astype(BF16)

        return body

    def state_body(order):
        def body(r):
            r.wait("zr")
            ham = ham_full(r)
            r.wait("pr")
            state = next_state(r, ham, surface_of(r), order)
            if order == 4:
                r.wait("s0", "s1", "s2")
                r.full[...] = state + r.state[...] + r.s2[...] + r.s1[...] + r.s0[...]
                for x in range(4):
                    for comp in range(2):
                        for q in range(4):
                            at = comp * 8 + q * 2
                            r.sum_o[x, comp, :, q * 512 : (q + 1) * 512] = r.full[at : at + 2, :]
                return
            r.state_o[...] = state
            first_out(r, r.u[8:9, :], r.u[88:89, :])
            r.wait("ham")
            ham_rows(r, state)
            z_out(r)

        return body

    for order in range(1, 5):
        zr = over_z(out["zo"])
        ys = lax.all_gather(out["low_o"], "chan", axis=0)
        part = call(
            surface_body, {**common, "state": inner[-1], "zr": zr, "amp": amp}, {"po": ((8, 32, 512), BF16)},
            surface_scratch, 1_500_000_000
        )["po"]
        pr = lax.all_to_all(part, "chan", 0, 0)
        ins = {**common, "ys": ys, "dipole": dipole, "field": strength, "pot": pot, "pr": pr, "amp": amp, "u": outer[-1]}
        inner_ins = {"info": info, "zr": zr, "pr": pr, "state": inner[-1]}
        if order < 4:
            outs = {"u_o": outer_spec, "low_o": low_spec}
            out = call(outer_body(order), ins, outs, outer_scratch, 4_000_000_000)
            outer.append(out["u_o"])
            inner_ins.update(ham=hams, u=out["u_o"])
            outs = {"zo": z_spec, "state_o": inner_spec}
            out.update(call(state_body(order), inner_ins, outs, {**full_scratch, **z_scratch}, 1_000_000_000))
            inner.append(out["state_o"])
        else:
            for i in range(3):
                ins["u%d" % i] = outer[i]
                inner_ins["s%d" % i] = inner[i]
            total = call(
                state_body(order), inner_ins, {"sum_o": ((4, 2, 2, 2048), F32)}, full_scratch, 1_000_000_000
            )["sum_o"]
            outs = {"psi_o": ((2, 64, 512), F32), "mark_o": ((2, 8, 128), F32)}
            out = call(outer_body(order), ins, outs, outer_scratch, 4_000_000_000)


    def finish(r):
        r.wait("sums")
        r.state_o[...] = r.sums[0]

    state_next = call(
        finish, {"sums": over_x(total), "mark": out["mark_o"]}, {"state_o": ((2, 2, 2048), F32)}, {}, 1_000_000
    )["state_o"]
    return out["psi_o"].transpose(0, 2, 1), state_next


def solution(mesh):
    return jax.shard_map(
        shards,
        mesh=mesh,
        in_specs=(
            P(None, "chan", "sector"),
            P("chan", "sector"),
            P("chan", None, None, None),
            P("chan", None),
            P("chan", None),
            P("chan"),
            P("chan"),
            P("chan", "sector", None),
            P(None, "chan", None),
            P(),
        ),
        out_specs=(P(None, "chan", "sector"), P(None, "chan", None)),
        check_vma=False,
    )
```

```python
import itertools
from types import SimpleNamespace

import jax
import jax.numpy as jnp
from jax import lax
from jax.experimental import pallas as pl
from jax.experimental.pallas import tpu as pltpu
from jax.sharding import PartitionSpec as P


F32 = jnp.float32
BF16 = jnp.bfloat16
VMEM = pltpu.VMEM
SMEM = pltpu.SMEM
KINETIC = 1.0 / 48.0


KEPT = ("after", "u", "local", "rows", "more", "state", "ham", "mark")
BIG = ("amp", "dipole", "keep_ham", "ys", "spread_ham")


def call(body, ins, outs, scratch, flops):
    arrays = dict(ins)
    scratch = dict(scratch)
    for name, value in arrays.items():
        if name not in ("info", "field") + KEPT and not name.startswith(("keep_", "spread_")):
            scratch[name + "_v"] = VMEM(value.shape, value.dtype)
    scratch["info_s"] = SMEM((128,), jnp.int32)
    scratch["field_s"] = SMEM((128,), F32)
    parts = {name: 4 if name in BIG else 1 for name in arrays if name not in KEPT}
    first_sem = dict(zip(parts, itertools.accumulate([0] + list(parts.values()))))
    scratch["sem"] = pltpu.SemaphoreType.DMA((sum(parts.values()),))
    names = [name if name in KEPT else "hbm_" + name for name in arrays] + list(outs) + list(scratch)

    def kernel(*refs):
        r = SimpleNamespace(**dict(zip(names, refs)))
        copies = {}

        def target(name):
            if name.startswith(("keep_", "spread_")):
                return getattr(r, name.split("_")[1] + "_o")
            return getattr(r, name + ("_s" if name in ("info", "field") else "_v"))

        def start(name):
            source, dest = getattr(r, "hbm_" + name), target(name)
            views = [(source, dest)]
            if name == "dipole":
                views = [(source.at[b, pl.ds(j, 4)], dest.at[b, pl.ds(j, 4)]) for b in range(2) for j in (0, 4)]
            elif name == "amp":
                views = [(source.at[:, pl.ds(q * 512, 512)], dest.at[:, pl.ds(q * 512, 512)]) for q in range(4)]
            elif name == "spread_ham":
                views = [(source, dest.at[x]) for x in range(4)]
            elif name in BIG:
                size = source.shape[0] // 4
                views = [(source.at[pl.ds(i * size, size)], dest.at[pl.ds(i * size, size)]) for i in range(4)]
            copies[name] = [
                pltpu.make_async_copy(view[0], view[1], r.sem.at[first_sem[name] + i]) for i, view in enumerate(views)
            ]
            for copy in copies[name]:
                copy.start()

        def wait(*wanted):
            for name in wanted:
                if name in copies:
                    for copy in copies.pop(name):
                        if copy is not None:
                            copy.wait()
                    setattr(r, name, target(name))

        def part(name, i):
            copies[name][i].wait()
            copies[name][i] = None

        r.wait = wait
        r.part = part
        for name in arrays:
            if name not in KEPT:
                start(name)
        body(r)
        wait(*list(copies))

    results = pl.pallas_call(
        kernel,
        out_shape=[jax.ShapeDtypeStruct(shape, kind) for shape, kind in outs.values()],
        in_specs=[pl.BlockSpec(memory_space=VMEM if name in KEPT else pltpu.HBM) for name in arrays],
        out_specs=[pl.BlockSpec(memory_space=VMEM) for _ in outs],
        scratch_shapes=list(scratch.values()),
        compiler_params=pltpu.CompilerParams(vmem_limit_bytes=52 * 1024 * 1024),
        cost_estimate=pl.CostEstimate(flops=flops, bytes_accessed=1024, transcendentals=0),
    )(*arrays.values())
    return dict(zip(outs, results))


def dot_t(a, b):
    return lax.dot_general(a, b, (((1,), (1,)), ((), ())), preferred_element_type=F32)


def dot(a, b):
    return lax.dot_general(a, b, (((1,), (0,)), ((), ())), preferred_element_type=F32)


def split(value):
    high = value.astype(BF16)
    return high, (value - high.astype(F32)).astype(BF16)


def rows_of(shape):
    return lax.broadcasted_iota(jnp.int32, shape, 0)


def ghost_of(r):
    states = jnp.concatenate([r.pr[c, 16:32, :] for c in range(8)], axis=0)
    row = rows_of((128, 512))
    quarter = (row >> 1) & 3
    total = jnp.zeros((128, 512), F32)
    for q in range(4):
        r.part("amp", q)
        part = dot_t(states, r.amp_v[:, q * 512 : (q + 1) * 512])
        total = total + jnp.where(quarter == q, part, 0.0)
    block = (row >> 4) * 2 + (row & 1)
    total = jnp.where(block == r.sym[...], total, 0.0)
    comp = (row >> 3) & 1
    g0 = jnp.sum(jnp.where(comp == 0, total, 0.0), axis=0, keepdims=True)
    g1 = jnp.sum(jnp.where(comp == 1, total, 0.0), axis=0, keepdims=True)
    return g0, g1


def surface_part(r, first0, first1):
    row = rows_of((32, 512))
    block = (row >> 2) * 2 + (row & 1)
    chosen = jnp.where(block == r.sym[...], jnp.where(((row >> 1) & 1) == 0, first0, first1), 0.0)
    both = jnp.concatenate(split(chosen), axis=0)
    for q in range(4):
        r.part("amp", q)
        part = dot(both, r.amp_v[:, q * 512 : (q + 1) * 512])
        r.sum[...] = part[:32] + part[32:]
        for c in range(8):
            for comp in range(2):
                at = c * 16 + comp * 8 + q * 2
                r.terms[at : at + 2, :] = r.sum[c * 4 + comp * 2 : c * 4 + comp * 2 + 2, :]


def surface_of(r):
    total = r.pr[0, 0:16, :].astype(F32)
    for c in range(1, 8):
        total = total + r.pr[c, 0:16, :].astype(F32)
    return total


def mask_of(r):
    r.wait("info")
    row = rows_of((16, 512))
    lane = lax.broadcasted_iota(jnp.int32, (16, 512), 1)
    size = jnp.where((row & 1) == 0, r.info[16], r.info[17])
    return (((row >> 1) & 3) * 512 + lane) < size


def ham_full(r):
    for z in range(16):
        for comp in range(2):
            at = comp * 8 + (z // 4) * 2
            for block in range(2):
                lanes = (comp * 2 + block) * 128
                r.full[at + block : at + block + 1, (z % 4) * 128 : (z % 4 + 1) * 128] = r.zr[z, :, lanes : lanes + 128]
    return r.full[...]


def next_state(r, ham, surface, order):
    image = jnp.where(mask_of(r), ham + surface, 0.0)
    return jnp.concatenate([image[8:], -image[:8]], axis=0) * (1.0 / order)


def first_received(r):
    return r.zr[0, :, 512:1024], r.zr[0, :, 1024:1536]


def ham_rows(r, state, out):
    both = jnp.concatenate(split(state), axis=0)
    row = rows_of((16, 128))
    total = jnp.zeros((16, 128), F32)
    for block in range(2):
        for q in range(4):
            ham = jnp.concatenate([r.ham[x, block, :, q * 512 : (q + 1) * 512] for x in range(4)], axis=0)
            part = dot_t(both, ham)
            keep = (((row >> 1) & 3) == q) & ((row & 1) == block)
            total = total + jnp.where(keep, part[:16] + part[16:], 0.0)
    r.sums[...] = total
    for comp in range(2):
        for block in range(2):
            at = comp * 8 + block
            rows = [r.sums[at + 2 * q : at + 2 * q + 1, :] for q in range(4)]
            lanes = (comp * 2 + block) * 128
            out[:, lanes : lanes + 128] = (rows[0] + rows[1]) + (rows[2] + rows[3])


def first_out(r, first0, first1):
    r.piece[:, 512:1024] = first0
    r.piece[:, 1024:1536] = first1


def z_out(r):
    piece = r.piece[...]
    for z in range(16):
        r.zo[z] = piece


def dipole_image(r):
    r.wait("info")
    for b in range(2):
        total = None
        for j in range(8):
            if j % 4 == 0:
                r.part("dipole", b * 2 + j // 4)
            n = r.info[b * 8 + j]
            lanes = pl.ds(pl.multiple_of((n & 1) * 256, 256), 256)
            part = dot_t(r.ys[n >> 1, 0:160, lanes], r.dipole_v[b, j])
            total = part if total is None else total + part
        r.dip[:, b * 256 : (b + 1) * 256] = total


def local_term(r, order):
    r.wait("info")
    images = []
    point = r.info[18] * 64 + rows_of((80, 512)) - 8
    for comp in range(2):
        u = r.u[comp * 80 : (comp + 1) * 80, :]
        r.pad[comp, 0:8, :] = jnp.zeros((8, 512), F32)
        r.pad[comp, 8:88, :] = u
        r.pad[comp, 88:96, :] = jnp.zeros((8, 512), F32)
        stencil = 16.0 * (r.pad[comp, 7:87, :] + r.pad[comp, 9:89, :]) - 30.0 * u
        stencil = stencil - (r.pad[comp, 6:86, :] + r.pad[comp, 10:90, :])
        image = -KINETIC * stencil + r.pot[...] * u
        images.append(jnp.where((point >= 0) & (point < r.all_points), image, 0.0))
    return images[1] * (1.0 / order), images[0] * (-1.0 / order)


def dipole_term(r, order):
    r.wait("info")
    point = r.info[18] * 64 + rows_of((80, 512)) - 8
    factor = r.field[0] * (1.0 / order) * ((point + 1).astype(F32) * (1.0 / r.all_points))
    return factor * r.dip[80:160, :], -factor * r.dip[0:80, :]


def ghost_term(r, order):
    r.wait("info")
    row = rows_of((8, 512))
    hub = jnp.where(r.info[18] == 0, 1.0 / order, 0.0).astype(F32)
    images = []
    for ghost in ghost_of(r):
        ghost = ghost * hub
        images.append(jnp.where(row == 0, (-15.0 * KINETIC) * ghost, jnp.where(row == 1, KINETIC * ghost, 0.0)))
    return images[1], -images[0]


def shards(psi, potential, dipole, coupling, amp, sym, sizes, inner_ham, inner_state, field):
    n_sector = lax.axis_size("sector")
    sector = lax.axis_index("sector")
    all_points = 64 * n_sector
    x_groups = [[z * 4 + x for x in range(4)] for z in range(16)]
    z_groups = [[z * 4 + x for z in range(16)] for x in range(4)]
    up = [(i, i + 1) for i in range(n_sector - 1)]
    down = [(i + 1, i) for i in range(n_sector - 1)]

    info = jnp.concatenate([coupling.reshape(16), sizes, sector[None].astype(jnp.int32), jnp.zeros((109,), jnp.int32)])
    common = {"info": info, "sym": sym.reshape(1, 512)}
    strength = jnp.broadcast_to(field, (128,))

    def over_z(piece):
        return lax.all_to_all(piece, "sector", 0, 0, axis_index_groups=z_groups)

    def over_x(piece):
        return lax.all_to_all(piece, "sector", 0, 0, axis_index_groups=x_groups)

    low_spec = ((160, 512), BF16)
    z_spec = ((16, 1, 1536), F32)
    outer_spec = ((160, 512), F32)
    inner_spec = ((16, 512), F32)
    end_spec = ((24, 512), F32)
    z_scratch = {"sums": VMEM((16, 128), F32), "piece": VMEM((1, 1536), F32)}
    surface_scratch = {"sum": VMEM((32, 512), F32), "terms": VMEM((128, 512), F32)}
    full_scratch = {"full": VMEM((16, 512), F32)}
    dipole_scratch = {"dip": VMEM((160, 512), F32)}
    local_scratch = {"pad": VMEM((2, 96, 512), F32)}


    def ends(r):
        r.wait("psi", "pot")
        for comp in range(2):
            r.head[comp * 8 : (comp + 1) * 8, :] = r.psi[comp, 0:8, :]
            r.tail[comp * 8 : (comp + 1) * 8, :] = r.psi[comp, 56:64, :]
        r.head[16:24, :] = r.pot[0:8, :].astype(F32)
        r.tail[16:24, :] = r.pot[56:64, :].astype(F32)

    own = {"psi": psi.transpose(0, 2, 1), "pot": potential.T}
    spread = call(lambda r: None, {"spread_ham": inner_ham}, {"ham_o": ((4,) + inner_ham.shape, BF16)}, {}, 1_000_000)
    out = call(ends, own, {"head": end_spec, "tail": end_spec}, {}, 1_000_000)
    hams = over_x(spread["ham_o"])
    left = lax.ppermute(out["tail"], "sector", up)
    right = lax.ppermute(out["head"], "sector", down)

    def begin(r):
        r.wait("psi", "pot", "left", "right", "given")
        for comp in range(2):
            for q in range(4):
                at = comp * 8 + q * 2
                r.state_o[at : at + 2, :] = r.given[comp, :, q * 512 : (q + 1) * 512]
            at = comp * 80
            r.u_o[at : at + 8, :] = r.left[comp * 8 : (comp + 1) * 8, :]
            r.u_o[at + 8 : at + 72, :] = r.psi[comp]
            r.u_o[at + 72 : at + 80, :] = r.right[comp * 8 : (comp + 1) * 8, :]
        r.pot_o[0:8, :] = r.left[16:24, :]
        r.pot_o[8:72, :] = r.pot[...].astype(F32)
        r.pot_o[72:80, :] = r.right[16:24, :]
        r.low_o[...] = r.u_o[...].astype(BF16)
        state = jnp.where(mask_of(r), r.state_o[...], 0.0)
        r.state_o[...] = state
        first_out(r, r.u_o[8:9, :], r.u_o[88:89, :])
        r.wait("keep_ham")
        r.ham = r.ham_o
        ham_rows(r, state, r.piece)
        z_out(r)

    out = call(
        begin,
        {"info": info, **own, "left": left, "right": right, "given": inner_state, "keep_ham": hams},
        {"ham_o": (hams.shape, BF16), "u_o": outer_spec, "pot_o": ((80, 512), F32), "state_o": inner_spec, "low_o": low_spec, "zo": z_spec},
        z_scratch, 1_000_000_000,
    )
    outer = [out["u_o"]]
    inner = [out["state_o"]]
    pot = out["pot_o"]
    hams = out["ham_o"]


    def surface_body(r):
        for c in range(8):
            r.po[c, 16:32, :] = r.state[...].astype(BF16)
        r.wait("zr", "sym")
        surface_part(r, *first_received(r))
        for c in range(8):
            r.po[c, 0:16, :] = r.terms[c * 16 : (c + 1) * 16, :].astype(BF16)

    def ghost_out(r, order):
        r.wait("pr", "sym")
        more = ghost_term(r, order)
        for comp in range(2):
            r.more_o[comp] = more[comp]

    def middle_body(order):
        def body(r):
            r.all_points = all_points
            r.wait("zr", "pr")
            state = next_state(r, ham_full(r), surface_of(r), order)
            if order == 4:
                r.wait("s0", "s1", "s2")
                r.full[...] = state + r.state[...] + r.s2[...] + r.s1[...] + r.s0[...]
                for x in range(4):
                    for comp in range(2):
                        for q in range(4):
                            at = comp * 8 + q * 2
                            r.sum_o[x, comp, :, q * 512 : (q + 1) * 512] = r.full[at : at + 2, :]
                ghost_out(r, order)
                return
            r.state_o[...] = state
            ham_rows(r, state, r.rows_o)
            ghost_out(r, order)

        return body

    def local_body(order):
        def body(r):
            r.all_points = all_points
            r.wait("pot")
            term = local_term(r, order)
            for comp in range(2):
                r.local_o[comp * 80 : (comp + 1) * 80, :] = term[comp]
            if order == 4:
                r.wait("u0", "u1", "u2")
                r.local_o[...] = r.local_o[...] + r.u0[...] + r.u1[...] + r.u2[...] + r.u[...]

        return body

    def dipole_body(order):
        def body(r):
            r.all_points = all_points
            r.wait("ys", "field")
            dipole_image(r)
            term = dipole_term(r, order)
            for comp in range(2):
                at = slice(comp * 80 + 8, comp * 80 + 16)
                r.dip[at, :] = term[comp][8:16, :] + r.more[comp]
            for comp in range(2):
                at = comp * 80
                if order == 4:
                    r.psi_o[comp, 0:8, :] = r.local[at + 8 : at + 16, :] + r.dip[at + 8 : at + 16, :]
                    r.psi_o[comp, 8:64, :] = r.local[at + 16 : at + 72, :] + term[comp][16:72, :]
                    r.mark_o[comp] = term[comp][0:8, 0:128]
                else:
                    total = r.local[at : at + 80, :] + term[comp]
                    r.u_o[at : at + 80, :] = total
                    r.u_o[at + 8 : at + 16, :] = r.local[at + 8 : at + 16, :] + r.dip[at + 8 : at + 16, :]
                    r.low_o[at : at + 80, :] = r.u_o[at : at + 80, :].astype(BF16)
            if order < 4:
                first_out(r, r.u_o[8:9, :], r.u_o[88:89, :])
                r.piece[:, 0:512] = r.rows[...]
                z_out(r)

        return body

    for order in range(1, 5):
        zr = over_z(out["zo"])
        ys = lax.all_gather(out["low_o"], "chan", axis=0)
        local_ins = {"info": info, "pot": pot, "u": outer[-1]}
        if order == 4:
            local_ins.update(u0=outer[0], u1=outer[1], u2=outer[2])
        local = call(local_body(order), local_ins, {"local_o": outer_spec}, local_scratch, 1_000_000_000)["local_o"]
        part = call(
            surface_body, {"sym": common["sym"], "after": local, "state": inner[-1], "zr": zr, "amp": amp}, {"po": ((8, 32, 512), BF16)},
            surface_scratch, 1_500_000_000
        )["po"]
        pr = lax.all_to_all(part, "chan", 0, 0)
        inner_ins = {"info": info, "zr": zr, "pr": pr, "state": inner[-1]}
        ghost_ins = {**common, "pr": pr, "amp": amp}
        if order == 4:
            for i in range(3):
                inner_ins["s%d" % i] = inner[i]
        ins = {"info": info, "ys": ys, "dipole": dipole, "field": strength, "local": local}
        more_spec = ((2, 8, 512), F32)
        if order < 4:
            outs = {"state_o": inner_spec, "rows_o": ((1, 512), F32), "more_o": more_spec}
            part = call(
                middle_body(order), {**inner_ins, **ghost_ins, "ham": hams}, outs, {**full_scratch, **z_scratch}, 2_000_000_000
            )
            inner.append(part["state_o"])
            ins.update(more=part["more_o"], rows=part["rows_o"])
            outs = {"zo": z_spec, "u_o": outer_spec, "low_o": low_spec}
            out = call(dipole_body(order), ins, outs, {**dipole_scratch, **z_scratch}, 4_000_000_000)
            outer.append(out["u_o"])
        else:
            outs = {"sum_o": ((4, 2, 2, 2048), F32), "more_o": more_spec}
            part = call(middle_body(4), {**inner_ins, **ghost_ins}, outs, full_scratch, 2_000_000_000)
            total = part["sum_o"]
            ins["more"] = part["more_o"]
            outs = {"psi_o": ((2, 64, 512), F32), "mark_o": ((2, 8, 128), F32)}
            out = call(dipole_body(4), ins, outs, dipole_scratch, 4_000_000_000)


    def finish(r):
        r.wait("sums")
        r.state_o[...] = r.sums[0]

    state_next = call(
        finish, {"sums": over_x(total), "mark": out["mark_o"]}, {"state_o": ((2, 2, 2048), F32)}, {}, 1_000_000
    )["state_o"]
    return out["psi_o"].transpose(0, 2, 1), state_next


def solution(mesh):
    return jax.shard_map(
        shards,
        mesh=mesh,
        in_specs=(
            P(None, "chan", "sector"),
            P("chan", "sector"),
            P("chan", None, None, None),
            P("chan", None),
            P("chan", None),
            P("chan"),
            P("chan"),
            P("chan", "sector", None),
            P(None, "chan", None),
            P(),
        ),
        out_specs=(P(None, "chan", "sector"), P(None, "chan", None)),
        check_vma=False,
    )
```

```python
import itertools
from types import SimpleNamespace

import jax
import jax.numpy as jnp
from jax import lax
from jax.experimental import pallas as pl
from jax.experimental.pallas import tpu as pltpu
from jax.sharding import PartitionSpec as P


F32 = jnp.float32
BF16 = jnp.bfloat16
VMEM = pltpu.VMEM
SMEM = pltpu.SMEM
KINETIC = 1.0 / 48.0


KEPT = ("after", "u", "local", "rows", "more", "state", "ham", "mark")
BIG = ("amp", "dipole", "keep_ham", "ys", "spread_ham")


def call(body, ins, outs, scratch, flops):
    arrays = dict(ins)
    scratch = dict(scratch)
    for name, value in arrays.items():
        if name not in ("info", "field") + KEPT and not name.startswith(("keep_", "spread_")):
            scratch[name + "_v"] = VMEM(value.shape, value.dtype)
    scratch["info_s"] = SMEM((128,), jnp.int32)
    scratch["field_s"] = SMEM((128,), F32)
    parts = {name: 4 if name in BIG else 1 for name in arrays if name not in KEPT}
    first_sem = dict(zip(parts, itertools.accumulate([0] + list(parts.values()))))
    scratch["sem"] = pltpu.SemaphoreType.DMA((sum(parts.values()),))
    names = [name if name in KEPT else "hbm_" + name for name in arrays] + list(outs) + list(scratch)

    def kernel(*refs):
        r = SimpleNamespace(**dict(zip(names, refs)))
        copies = {}

        def target(name):
            if name.startswith(("keep_", "spread_")):
                return getattr(r, name.split("_")[1] + "_o")
            return getattr(r, name + ("_s" if name in ("info", "field") else "_v"))

        def start(name):
            source, dest = getattr(r, "hbm_" + name), target(name)
            views = [(source, dest)]
            if name == "dipole":
                views = [(source.at[b, pl.ds(j, 4)], dest.at[b, pl.ds(j, 4)]) for b in range(2) for j in (0, 4)]
            elif name == "amp":
                views = [(source.at[:, pl.ds(q * 512, 512)], dest.at[:, pl.ds(q * 512, 512)]) for q in range(4)]
            elif name == "spread_ham":
                views = [(source, dest.at[x]) for x in range(4)]
            elif name in BIG:
                size = source.shape[0] // 4
                views = [(source.at[pl.ds(i * size, size)], dest.at[pl.ds(i * size, size)]) for i in range(4)]
            copies[name] = [
                pltpu.make_async_copy(view[0], view[1], r.sem.at[first_sem[name] + i]) for i, view in enumerate(views)
            ]
            for copy in copies[name]:
                copy.start()

        def wait(*wanted):
            for name in wanted:
                if name in copies:
                    for copy in copies.pop(name):
                        if copy is not None:
                            copy.wait()
                    setattr(r, name, target(name))

        def part(name, i):
            copies[name][i].wait()
            copies[name][i] = None

        r.wait = wait
        r.part = part
        for name in arrays:
            if name not in KEPT:
                start(name)
        body(r)
        wait(*list(copies))

    results = pl.pallas_call(
        kernel,
        out_shape=[jax.ShapeDtypeStruct(shape, kind) for shape, kind in outs.values()],
        in_specs=[pl.BlockSpec(memory_space=VMEM if name in KEPT else pltpu.HBM) for name in arrays],
        out_specs=[pl.BlockSpec(memory_space=VMEM) for _ in outs],
        scratch_shapes=list(scratch.values()),
        compiler_params=pltpu.CompilerParams(vmem_limit_bytes=52 * 1024 * 1024),
        cost_estimate=pl.CostEstimate(flops=flops, bytes_accessed=1024, transcendentals=0),
    )(*arrays.values())
    return dict(zip(outs, results))


def dot_t(a, b):
    return lax.dot_general(a, b, (((1,), (1,)), ((), ())), preferred_element_type=F32)


def dot(a, b):
    return lax.dot_general(a, b, (((1,), (0,)), ((), ())), preferred_element_type=F32)


def split(value):
    high = value.astype(BF16)
    return high, (value - high.astype(F32)).astype(BF16)


def rows_of(shape):
    return lax.broadcasted_iota(jnp.int32, shape, 0)


def ghost_of(r):
    states = jnp.concatenate([r.pr[c, 16:32, :] for c in range(8)], axis=0)
    row = rows_of((128, 512))
    quarter = (row >> 1) & 3
    total = jnp.zeros((128, 512), F32)
    for q in range(4):
        r.part("amp", q)
        part = dot_t(states, r.amp_v[:, q * 512 : (q + 1) * 512])
        total = total + jnp.where(quarter == q, part, 0.0)
    block = (row >> 4) * 2 + (row & 1)
    total = jnp.where(block == r.sym[...], total, 0.0)
    comp = (row >> 3) & 1
    g0 = jnp.sum(jnp.where(comp == 0, total, 0.0), axis=0, keepdims=True)
    g1 = jnp.sum(jnp.where(comp == 1, total, 0.0), axis=0, keepdims=True)
    return g0, g1


def surface_part(r, first0, first1):
    row = rows_of((32, 512))
    block = (row >> 2) * 2 + (row & 1)
    chosen = jnp.where(block == r.sym[...], jnp.where(((row >> 1) & 1) == 0, first0, first1), 0.0)
    both = jnp.concatenate(split(chosen), axis=0)
    for q in range(4):
        r.part("amp", q)
        part = dot(both, r.amp_v[:, q * 512 : (q + 1) * 512])
        r.sum[...] = part[:32] + part[32:]
        for c in range(8):
            for comp in range(2):
                at = c * 16 + comp * 8 + q * 2
                r.terms[at : at + 2, :] = r.sum[c * 4 + comp * 2 : c * 4 + comp * 2 + 2, :]


def surface_of(r):
    total = r.pr[0, 0:16, :].astype(F32)
    for c in range(1, 8):
        total = total + r.pr[c, 0:16, :].astype(F32)
    return total


def mask_of(r):
    r.wait("info")
    row = rows_of((16, 512))
    lane = lax.broadcasted_iota(jnp.int32, (16, 512), 1)
    size = jnp.where((row & 1) == 0, r.info[16], r.info[17])
    return (((row >> 1) & 3) * 512 + lane) < size


def ham_full(r):
    for z in range(16):
        for comp in range(2):
            at = comp * 8 + (z // 4) * 2
            for block in range(2):
                lanes = (comp * 2 + block) * 128
                r.full[at + block : at + block + 1, (z % 4) * 128 : (z % 4 + 1) * 128] = r.zr[z, :, lanes : lanes + 128]
    return r.full[...]


def next_state(r, ham, surface, order):
    image = jnp.where(mask_of(r), ham + surface, 0.0)
    return jnp.concatenate([image[8:], -image[:8]], axis=0) * (1.0 / order)


def first_received(r):
    return r.zr[0, :, 512:1024], r.zr[0, :, 1024:1536]


def ham_rows(r, state, out):
    both = jnp.concatenate(split(state), axis=0)
    row = rows_of((16, 128))
    total = jnp.zeros((16, 128), F32)
    for block in range(2):
        for q in range(4):
            ham = jnp.concatenate([r.ham[x, block, :, q * 512 : (q + 1) * 512] for x in range(4)], axis=0)
            part = dot_t(both, ham)
            keep = (((row >> 1) & 3) == q) & ((row & 1) == block)
            total = total + jnp.where(keep, part[:16] + part[16:], 0.0)
    r.sums[...] = total
    for comp in range(2):
        for block in range(2):
            at = comp * 8 + block
            rows = [r.sums[at + 2 * q : at + 2 * q + 1, :] for q in range(4)]
            lanes = (comp * 2 + block) * 128
            out[:, lanes : lanes + 128] = (rows[0] + rows[1]) + (rows[2] + rows[3])


def first_out(r, first0, first1):
    r.piece[:, 512:1024] = first0
    r.piece[:, 1024:1536] = first1


def z_out(r):
    piece = r.piece[...]
    for z in range(16):
        r.zo[z] = piece


def dipole_image(r):
    r.wait("info")
    for b in range(2):
        total = None
        for j in range(8):
            if j % 4 == 0:
                r.part("dipole", b * 2 + j // 4)
            n = r.info[b * 8 + j]
            lanes = pl.ds(pl.multiple_of((n & 1) * 256, 256), 256)
            part = dot_t(r.ys[n >> 1, 0:160, lanes], r.dipole_v[b, j])
            total = part if total is None else total + part
        r.dip[:, b * 256 : (b + 1) * 256] = total


def local_term(r, order):
    r.wait("info")
    images = []
    point = r.info[18] * 64 + rows_of((80, 512)) - 8
    for comp in range(2):
        u = r.u[comp * 80 : (comp + 1) * 80, :]
        r.pad[comp, 0:8, :] = jnp.zeros((8, 512), F32)
        r.pad[comp, 8:88, :] = u
        r.pad[comp, 88:96, :] = jnp.zeros((8, 512), F32)
        stencil = 16.0 * (r.pad[comp, 7:87, :] + r.pad[comp, 9:89, :]) - 30.0 * u
        stencil = stencil - (r.pad[comp, 6:86, :] + r.pad[comp, 10:90, :])
        image = -KINETIC * stencil + r.pot[...] * u
        images.append(jnp.where((point >= 0) & (point < r.all_points), image, 0.0))
    return images[1] * (1.0 / order), images[0] * (-1.0 / order)


def dipole_term(r, order):
    r.wait("info")
    point = r.info[18] * 64 + rows_of((80, 512)) - 8
    factor = r.field[0] * (1.0 / order) * ((point + 1).astype(F32) * (1.0 / r.all_points))
    return factor * r.dip[80:160, :], -factor * r.dip[0:80, :]


def ghost_term(r, order):
    r.wait("info")
    row = rows_of((8, 512))
    images = []
    for ghost in ghost_of(r):
        ghost = jnp.where(r.info[18] == 0, ghost * (1.0 / order), 0.0)
        images.append(jnp.where(row == 0, (-15.0 * KINETIC) * ghost, jnp.where(row == 1, KINETIC * ghost, 0.0)))
    return images[1], -images[0]


def shards(psi, potential, dipole, coupling, amp, sym, sizes, inner_ham, inner_state, field):
    n_sector = lax.axis_size("sector")
    sector = lax.axis_index("sector")
    all_points = 64 * n_sector
    x_groups = [[z * 4 + x for x in range(4)] for z in range(16)]
    z_groups = [[z * 4 + x for z in range(16)] for x in range(4)]
    up = [(i, i + 1) for i in range(n_sector - 1)]
    down = [(i + 1, i) for i in range(n_sector - 1)]

    info = jnp.concatenate([coupling.reshape(16), sizes, sector[None].astype(jnp.int32), jnp.zeros((109,), jnp.int32)])
    common = {"info": info, "sym": sym.reshape(1, 512)}
    strength = jnp.broadcast_to(field, (128,))

    def over_z(piece):
        return lax.all_to_all(piece, "sector", 0, 0, axis_index_groups=z_groups)

    def over_x(piece):
        return lax.all_to_all(piece, "sector", 0, 0, axis_index_groups=x_groups)

    low_spec = ((160, 512), BF16)
    z_spec = ((16, 1, 1536), F32)
    outer_spec = ((160, 512), F32)
    inner_spec = ((16, 512), F32)
    end_spec = ((24, 512), F32)
    z_scratch = {"sums": VMEM((16, 128), F32), "piece": VMEM((1, 1536), F32)}
    surface_scratch = {"sum": VMEM((32, 512), F32), "terms": VMEM((128, 512), F32)}
    full_scratch = {"full": VMEM((16, 512), F32)}
    dipole_scratch = {"dip": VMEM((160, 512), F32)}
    local_scratch = {"pad": VMEM((2, 96, 512), F32)}


    def ends(r):
        r.wait("psi", "pot")
        for comp in range(2):
            r.head[comp * 8 : (comp + 1) * 8, :] = r.psi[comp, 0:8, :]
            r.tail[comp * 8 : (comp + 1) * 8, :] = r.psi[comp, 56:64, :]
        r.head[16:24, :] = r.pot[0:8, :].astype(F32)
        r.tail[16:24, :] = r.pot[56:64, :].astype(F32)

    own = {"psi": psi.transpose(0, 2, 1), "pot": potential.T}
    spread = call(lambda r: None, {"spread_ham": inner_ham}, {"ham_o": ((4,) + inner_ham.shape, BF16)}, {}, 1_000_000)
    out = call(ends, own, {"head": end_spec, "tail": end_spec}, {}, 1_000_000)
    hams = over_x(spread["ham_o"])
    left = lax.ppermute(out["tail"], "sector", up)
    right = lax.ppermute(out["head"], "sector", down)

    def begin(r):
        r.wait("psi", "pot", "left", "right", "given")
        for comp in range(2):
            for q in range(4):
                at = comp * 8 + q * 2
                r.state_o[at : at + 2, :] = r.given[comp, :, q * 512 : (q + 1) * 512]
            at = comp * 80
            r.u_o[at : at + 8, :] = r.left[comp * 8 : (comp + 1) * 8, :]
            r.u_o[at + 8 : at + 72, :] = r.psi[comp]
            r.u_o[at + 72 : at + 80, :] = r.right[comp * 8 : (comp + 1) * 8, :]
        r.pot_o[0:8, :] = r.left[16:24, :]
        r.pot_o[8:72, :] = r.pot[...].astype(F32)
        r.pot_o[72:80, :] = r.right[16:24, :]
        r.low_o[...] = r.u_o[...].astype(BF16)
        state = jnp.where(mask_of(r), r.state_o[...], 0.0)
        r.state_o[...] = state
        first_out(r, r.u_o[8:9, :], r.u_o[88:89, :])
        r.wait("keep_ham")
        r.ham = r.ham_o
        ham_rows(r, state, r.piece)
        z_out(r)

    out = call(
        begin,
        {"info": info, **own, "left": left, "right": right, "given": inner_state, "keep_ham": hams},
        {"ham_o": (hams.shape, BF16), "u_o": outer_spec, "pot_o": ((80, 512), F32), "state_o": inner_spec, "low_o": low_spec, "zo": z_spec},
        z_scratch, 1_000_000_000,
    )
    outer = [out["u_o"]]
    inner = [out["state_o"]]
    pot = out["pot_o"]
    hams = out["ham_o"]


    def surface_body(r):
        for c in range(8):
            r.po[c, 16:32, :] = r.state[...].astype(BF16)
        r.wait("zr", "sym")
        surface_part(r, *first_received(r))
        for c in range(8):
            r.po[c, 0:16, :] = r.terms[c * 16 : (c + 1) * 16, :].astype(BF16)

    def ghost_out(r, order):
        r.wait("pr", "sym")
        more = ghost_term(r, order)
        for comp in range(2):
            r.more_o[comp] = more[comp]

    def middle_body(order):
        def body(r):
            r.all_points = all_points
            r.wait("zr", "pr")
            state = next_state(r, ham_full(r), surface_of(r), order)
            if order == 4:
                r.wait("s0", "s1", "s2")
                r.full[...] = state + r.state[...] + r.s2[...] + r.s1[...] + r.s0[...]
                for x in range(4):
                    for comp in range(2):
                        for q in range(4):
                            at = comp * 8 + q * 2
                            r.sum_o[x, comp, :, q * 512 : (q + 1) * 512] = r.full[at : at + 2, :]
                ghost_out(r, order)
                return
            r.state_o[...] = state
            ham_rows(r, state, r.rows_o)
            ghost_out(r, order)

        return body

    def local_body(order):
        def body(r):
            r.all_points = all_points
            r.wait("pot")
            term = local_term(r, order)
            for comp in range(2):
                r.local_o[comp * 80 : (comp + 1) * 80, :] = term[comp]
            if order == 4:
                r.wait("u0", "u1", "u2")
                r.local_o[...] = r.local_o[...] + r.u0[...] + r.u1[...] + r.u2[...] + r.u[...]

        return body

    def dipole_body(order):
        def body(r):
            r.all_points = all_points
            r.wait("ys", "field")
            dipole_image(r)
            term = dipole_term(r, order)
            for comp in range(2):
                at = slice(comp * 80 + 8, comp * 80 + 16)
                r.dip[at, :] = term[comp][8:16, :] + r.more[comp]
            for comp in range(2):
                at = comp * 80
                if order == 4:
                    r.psi_o[comp, 0:8, :] = r.local[at + 8 : at + 16, :] + r.dip[at + 8 : at + 16, :]
                    r.psi_o[comp, 8:64, :] = r.local[at + 16 : at + 72, :] + term[comp][16:72, :]
                    r.mark_o[comp] = term[comp][0:8, 0:128]
                else:
                    total = r.local[at : at + 80, :] + term[comp]
                    r.u_o[at : at + 80, :] = total
                    r.u_o[at + 8 : at + 16, :] = r.local[at + 8 : at + 16, :] + r.dip[at + 8 : at + 16, :]
                    r.low_o[at : at + 80, :] = r.u_o[at : at + 80, :].astype(BF16)
            if order < 4:
                first_out(r, r.u_o[8:9, :], r.u_o[88:89, :])
                r.piece[:, 0:512] = r.rows[...]
                z_out(r)

        return body

    for order in range(1, 5):
        zr = over_z(out["zo"])
        ys = lax.all_gather(out["low_o"], "chan", axis=0)
        local_ins = {"info": info, "pot": pot, "u": outer[-1]}
        if order == 4:
            local_ins.update(u0=outer[0], u1=outer[1], u2=outer[2])
        local = call(local_body(order), local_ins, {"local_o": outer_spec}, local_scratch, 1_000_000_000)["local_o"]
        part = call(
            surface_body, {"sym": common["sym"], "after": local, "state": inner[-1], "zr": zr, "amp": amp}, {"po": ((8, 32, 512), BF16)},
            surface_scratch, 1_500_000_000
        )["po"]
        pr = lax.all_to_all(part, "chan", 0, 0)
        inner_ins = {"info": info, "zr": zr, "pr": pr, "state": inner[-1]}
        ghost_ins = {**common, "pr": pr, "amp": amp}
        if order == 4:
            for i in range(3):
                inner_ins["s%d" % i] = inner[i]
        ins = {"info": info, "ys": ys, "dipole": dipole, "field": strength, "local": local}
        more_spec = ((2, 8, 512), F32)
        if order < 4:
            outs = {"state_o": inner_spec, "rows_o": ((1, 512), F32), "more_o": more_spec}
            part = call(
                middle_body(order), {**inner_ins, **ghost_ins, "ham": hams}, outs, {**full_scratch, **z_scratch}, 2_000_000_000
            )
            inner.append(part["state_o"])
            ins.update(more=part["more_o"], rows=part["rows_o"])
            outs = {"zo": z_spec, "u_o": outer_spec, "low_o": low_spec}
            out = call(dipole_body(order), ins, outs, {**dipole_scratch, **z_scratch}, 4_000_000_000)
            outer.append(out["u_o"])
        else:
            outs = {"sum_o": ((4, 2, 2, 2048), F32), "more_o": more_spec}
            part = call(middle_body(4), {**inner_ins, **ghost_ins}, outs, full_scratch, 2_000_000_000)
            total = part["sum_o"]
            ins["more"] = part["more_o"]
            outs = {"psi_o": ((2, 64, 512), F32), "mark_o": ((2, 8, 128), F32)}
            out = call(dipole_body(4), ins, outs, dipole_scratch, 4_000_000_000)


    def finish(r):
        r.wait("sums")
        r.state_o[...] = r.sums[0]

    state_next = call(
        finish, {"sums": over_x(total), "mark": out["mark_o"]}, {"state_o": ((2, 2, 2048), F32)}, {}, 1_000_000
    )["state_o"]
    return out["psi_o"].transpose(0, 2, 1), state_next


def solution(mesh):
    return jax.shard_map(
        shards,
        mesh=mesh,
        in_specs=(
            P(None, "chan", "sector"),
            P("chan", "sector"),
            P("chan", None, None, None),
            P("chan", None),
            P("chan", None),
            P("chan"),
            P("chan"),
            P("chan", "sector", None),
            P(None, "chan", None),
            P(),
        ),
        out_specs=(P(None, "chan", "sector"), P(None, "chan", None)),
        check_vma=False,
    )
```

```python
import itertools
from types import SimpleNamespace

import jax
import jax.numpy as jnp
from jax import lax
from jax.experimental import pallas as pl
from jax.experimental.pallas import tpu as pltpu
from jax.sharding import PartitionSpec as P


F32 = jnp.float32
BF16 = jnp.bfloat16
VMEM = pltpu.VMEM
SMEM = pltpu.SMEM
KINETIC = 1.0 / 48.0


KEPT = ("after", "u", "local", "rows", "more", "state", "ham", "mark")
BIG = ("amp", "dipole", "keep_ham", "ys", "spread_ham")


def call(body, ins, outs, scratch, flops):
    arrays = dict(ins)
    scratch = dict(scratch)
    for name, value in arrays.items():
        if name not in ("info", "field") + KEPT and not name.startswith(("keep_", "spread_")):
            scratch[name + "_v"] = VMEM(value.shape, value.dtype)
    scratch["info_s"] = SMEM((128,), jnp.int32)
    scratch["field_s"] = SMEM((128,), F32)
    parts = {name: 4 if name in BIG else 1 for name in arrays if name not in KEPT}
    first_sem = dict(zip(parts, itertools.accumulate([0] + list(parts.values()))))
    scratch["sem"] = pltpu.SemaphoreType.DMA((sum(parts.values()),))
    names = [name if name in KEPT else "hbm_" + name for name in arrays] + list(outs) + list(scratch)

    def kernel(*refs):
        r = SimpleNamespace(**dict(zip(names, refs)))
        copies = {}

        def target(name):
            if name.startswith(("keep_", "spread_")):
                return getattr(r, name.split("_")[1] + "_o")
            return getattr(r, name + ("_s" if name in ("info", "field") else "_v"))

        def start(name):
            source, dest = getattr(r, "hbm_" + name), target(name)
            views = [(source, dest)]
            if name == "dipole":
                views = [(source.at[b, pl.ds(j, 4)], dest.at[b, pl.ds(j, 4)]) for b in range(2) for j in (0, 4)]
            elif name == "amp":
                views = [(source.at[:, pl.ds(q * 512, 512)], dest.at[:, pl.ds(q * 512, 512)]) for q in range(4)]
            elif name == "spread_ham":
                views = [(source, dest.at[x]) for x in range(4)]
            elif name in BIG:
                size = source.shape[0] // 4
                views = [(source.at[pl.ds(i * size, size)], dest.at[pl.ds(i * size, size)]) for i in range(4)]
            copies[name] = [
                pltpu.make_async_copy(view[0], view[1], r.sem.at[first_sem[name] + i]) for i, view in enumerate(views)
            ]
            for copy in copies[name]:
                copy.start()

        def wait(*wanted):
            for name in wanted:
                if name in copies:
                    for copy in copies.pop(name):
                        if copy is not None:
                            copy.wait()
                    setattr(r, name, target(name))

        def part(name, i):
            copies[name][i].wait()
            copies[name][i] = None

        r.wait = wait
        r.part = part
        for name in arrays:
            if name not in KEPT:
                start(name)
        body(r)
        wait(*list(copies))

    results = pl.pallas_call(
        kernel,
        out_shape=[jax.ShapeDtypeStruct(shape, kind) for shape, kind in outs.values()],
        in_specs=[pl.BlockSpec(memory_space=VMEM if name in KEPT else pltpu.HBM) for name in arrays],
        out_specs=[pl.BlockSpec(memory_space=VMEM) for _ in outs],
        scratch_shapes=list(scratch.values()),
        compiler_params=pltpu.CompilerParams(vmem_limit_bytes=52 * 1024 * 1024),
        cost_estimate=pl.CostEstimate(flops=flops, bytes_accessed=1024, transcendentals=0),
    )(*arrays.values())
    return dict(zip(outs, results))


def dot_t(a, b):
    return lax.dot_general(a, b, (((1,), (1,)), ((), ())), preferred_element_type=F32)


def dot(a, b):
    return lax.dot_general(a, b, (((1,), (0,)), ((), ())), preferred_element_type=F32)


def split(value):
    high = value.astype(BF16)
    return high, (value - high.astype(F32)).astype(BF16)


def rows_of(shape):
    return lax.broadcasted_iota(jnp.int32, shape, 0)


def ghost_of(r):
    states = jnp.concatenate([r.pr[c, 16:32, :] for c in range(8)], axis=0)
    row = rows_of((128, 512))
    quarter = (row >> 1) & 3
    total = jnp.zeros((128, 512), F32)
    for q in range(4):
        r.part("amp", q)
        part = dot_t(states, r.amp_v[:, q * 512 : (q + 1) * 512])
        total = total + jnp.where(quarter == q, part, 0.0)
    block = (row >> 4) * 2 + (row & 1)
    total = jnp.where(block == r.sym[...], total, 0.0)
    comp = (row >> 3) & 1
    g0 = jnp.sum(jnp.where(comp == 0, total, 0.0), axis=0, keepdims=True)
    g1 = jnp.sum(jnp.where(comp == 1, total, 0.0), axis=0, keepdims=True)
    return g0, g1


def surface_part(r, first0, first1):
    row = rows_of((32, 512))
    block = (row >> 2) * 2 + (row & 1)
    chosen = jnp.where(block == r.sym[...], jnp.where(((row >> 1) & 1) == 0, first0, first1), 0.0)
    both = jnp.concatenate(split(chosen), axis=0)
    for q in range(4):
        r.part("amp", q)
        part = dot(both, r.amp_v[:, q * 512 : (q + 1) * 512])
        r.sum[...] = part[:32] + part[32:]
        for c in range(8):
            for comp in range(2):
                at = c * 16 + comp * 8 + q * 2
                r.terms[at : at + 2, :] = r.sum[c * 4 + comp * 2 : c * 4 + comp * 2 + 2, :]


def surface_of(r):
    total = r.pr[0, 0:16, :].astype(F32)
    for c in range(1, 8):
        total = total + r.pr[c, 0:16, :].astype(F32)
    return total


def mask_of(r):
    r.wait("info")
    row = rows_of((16, 512))
    lane = lax.broadcasted_iota(jnp.int32, (16, 512), 1)
    size = jnp.where((row & 1) == 0, r.info[16], r.info[17])
    return (((row >> 1) & 3) * 512 + lane) < size


def ham_full(r):
    for z in range(16):
        for comp in range(2):
            at = comp * 8 + (z // 4) * 2
            for block in range(2):
                lanes = (comp * 2 + block) * 128
                r.full[at + block : at + block + 1, (z % 4) * 128 : (z % 4 + 1) * 128] = r.zr[z, :, lanes : lanes + 128]
    return r.full[...]


def next_state(r, ham, surface, order):
    image = jnp.where(mask_of(r), ham + surface, 0.0)
    return jnp.concatenate([image[8:], -image[:8]], axis=0) * (1.0 / order)


def first_received(r):
    return r.zr[0, :, 512:1024], r.zr[0, :, 1024:1536]


def ham_rows(r, state, out):
    both = jnp.concatenate(split(state), axis=0)
    row = rows_of((16, 128))
    total = jnp.zeros((16, 128), F32)
    for block in range(2):
        for q in range(4):
            ham = jnp.concatenate([r.ham[x, block, :, q * 512 : (q + 1) * 512] for x in range(4)], axis=0)
            part = dot_t(both, ham)
            keep = (((row >> 1) & 3) == q) & ((row & 1) == block)
            total = total + jnp.where(keep, part[:16] + part[16:], 0.0)
    r.sums[...] = total
    for comp in range(2):
        for block in range(2):
            at = comp * 8 + block
            rows = [r.sums[at + 2 * q : at + 2 * q + 1, :] for q in range(4)]
            lanes = (comp * 2 + block) * 128
            out[:, lanes : lanes + 128] = (rows[0] + rows[1]) + (rows[2] + rows[3])


def first_out(r, first0, first1):
    r.piece[:, 512:1024] = first0
    r.piece[:, 1024:1536] = first1


def z_out(r):
    piece = r.piece[...]
    for z in range(16):
        r.zo[z] = piece


def dipole_image(r):
    r.wait("info")
    for b in range(2):
        total = None
        for j in range(8):
            if j % 4 == 0:
                r.part("dipole", b * 2 + j // 4)
            n = r.info[b * 8 + j]
            lanes = pl.ds(pl.multiple_of((n & 1) * 256, 256), 256)
            part = dot_t(r.ys[n >> 1, 0:160, lanes], r.dipole_v[b, j])
            total = part if total is None else total + part
        r.dip[:, b * 256 : (b + 1) * 256] = total


def local_term(r, order):
    r.wait("info")
    images = []
    point = r.info[18] * 64 + rows_of((80, 512)) - 8
    for comp in range(2):
        u = r.u[comp * 80 : (comp + 1) * 80, :]
        r.pad[comp, 0:8, :] = jnp.zeros((8, 512), F32)
        r.pad[comp, 8:88, :] = u
        r.pad[comp, 88:96, :] = jnp.zeros((8, 512), F32)
        stencil = 16.0 * (r.pad[comp, 7:87, :] + r.pad[comp, 9:89, :]) - 30.0 * u
        stencil = stencil - (r.pad[comp, 6:86, :] + r.pad[comp, 10:90, :])
        image = -KINETIC * stencil + r.pot[...] * u
        images.append(jnp.where((point >= 0) & (point < r.all_points), image, 0.0))
    return images[1] * (1.0 / order), images[0] * (-1.0 / order)


def dipole_term(r, order):
    r.wait("info")
    point = r.info[18] * 64 + rows_of((80, 512)) - 8
    factor = r.field[0] * (1.0 / order) * ((point + 1).astype(F32) * (1.0 / r.all_points))
    return factor * r.dip[80:160, :], -factor * r.dip[0:80, :]


def ghost_term(r, order):
    r.wait("info")
    row = rows_of((8, 512))
    images = []
    for ghost in ghost_of(r):
        ghost = jnp.where(r.info[18] == 0, ghost * (1.0 / order), 0.0)
        images.append(jnp.where(row == 0, (-15.0 * KINETIC) * ghost, jnp.where(row == 1, KINETIC * ghost, 0.0)))
    return images[1], -images[0]


def shards(psi, potential, dipole, coupling, amp, sym, sizes, inner_ham, inner_state, field):
    n_sector = lax.axis_size("sector")
    sector = lax.axis_index("sector")
    all_points = 64 * n_sector
    x_groups = [[z * 4 + x for x in range(4)] for z in range(16)]
    z_groups = [[z * 4 + x for z in range(16)] for x in range(4)]
    up = [(i, i + 1) for i in range(n_sector - 1)]
    down = [(i + 1, i) for i in range(n_sector - 1)]

    info = jnp.concatenate([coupling.reshape(16), sizes, sector[None].astype(jnp.int32), jnp.zeros((109,), jnp.int32)])
    common = {"info": info, "sym": sym.reshape(1, 512)}
    strength = jnp.broadcast_to(field, (128,))

    def over_z(piece):
        return lax.all_to_all(piece, "sector", 0, 0, axis_index_groups=z_groups)

    def over_x(piece):
        return lax.all_to_all(piece, "sector", 0, 0, axis_index_groups=x_groups)

    low_spec = ((160, 512), BF16)
    z_spec = ((16, 1, 1536), F32)
    outer_spec = ((160, 512), F32)
    inner_spec = ((16, 512), F32)
    end_spec = ((24, 512), F32)
    z_scratch = {"sums": VMEM((16, 128), F32), "piece": VMEM((1, 1536), F32)}
    surface_scratch = {"sum": VMEM((32, 512), F32), "terms": VMEM((128, 512), F32)}
    full_scratch = {"full": VMEM((16, 512), F32)}
    dipole_scratch = {"dip": VMEM((160, 512), F32)}
    local_scratch = {"pad": VMEM((2, 96, 512), F32)}


    def ends(r):
        r.wait("psi", "pot")
        for comp in range(2):
            r.head[comp * 8 : (comp + 1) * 8, :] = r.psi[comp, 0:8, :]
            r.tail[comp * 8 : (comp + 1) * 8, :] = r.psi[comp, 56:64, :]
        r.head[16:24, :] = r.pot[0:8, :].astype(F32)
        r.tail[16:24, :] = r.pot[56:64, :].astype(F32)

    own = {"psi": psi.transpose(0, 2, 1), "pot": potential.T}
    spread = call(lambda r: None, {"spread_ham": inner_ham}, {"ham_o": ((4,) + inner_ham.shape, BF16)}, {}, 1_000_000)
    out = call(ends, own, {"head": end_spec, "tail": end_spec}, {}, 1_000_000)
    hams = over_x(spread["ham_o"])
    left = lax.ppermute(out["tail"], "sector", up)
    right = lax.ppermute(out["head"], "sector", down)

    def begin(r):
        r.wait("psi", "pot", "left", "right", "given")
        for comp in range(2):
            for q in range(4):
                at = comp * 8 + q * 2
                r.state_o[at : at + 2, :] = r.given[comp, :, q * 512 : (q + 1) * 512]
            at = comp * 80
            r.u_o[at : at + 8, :] = r.left[comp * 8 : (comp + 1) * 8, :]
            r.u_o[at + 8 : at + 72, :] = r.psi[comp]
            r.u_o[at + 72 : at + 80, :] = r.right[comp * 8 : (comp + 1) * 8, :]
        r.pot_o[0:8, :] = r.left[16:24, :]
        r.pot_o[8:72, :] = r.pot[...].astype(F32)
        r.pot_o[72:80, :] = r.right[16:24, :]
        r.low_o[...] = r.u_o[...].astype(BF16)
        state = jnp.where(mask_of(r), r.state_o[...], 0.0)
        r.state_o[...] = state
        first_out(r, r.u_o[8:9, :], r.u_o[88:89, :])
        r.wait("keep_ham")
        r.ham = r.ham_o
        ham_rows(r, state, r.piece)
        z_out(r)

    out = call(
        begin,
        {"info": info, **own, "left": left, "right": right, "given": inner_state, "keep_ham": hams},
        {"ham_o": (hams.shape, BF16), "u_o": outer_spec, "pot_o": ((80, 512), F32), "state_o": inner_spec, "low_o": low_spec, "zo": z_spec},
        z_scratch, 1_000_000_000,
    )
    outer = [out["u_o"]]
    inner = [out["state_o"]]
    pot = out["pot_o"]
    hams = out["ham_o"]


    def surface_body(r):
        for c in range(8):
            r.po[c, 16:32, :] = r.state[...].astype(BF16)
        r.wait("zr", "sym")
        surface_part(r, *first_received(r))
        for c in range(8):
            r.po[c, 0:16, :] = r.terms[c * 16 : (c + 1) * 16, :].astype(BF16)

    def ghost_out(r, order):
        r.wait("pr", "sym")
        more = ghost_term(r, order)
        for comp in range(2):
            r.more_o[comp] = more[comp]

    def middle_body(order):
        def body(r):
            r.all_points = all_points
            r.wait("zr", "pr")
            state = next_state(r, ham_full(r), surface_of(r), order)
            if order == 4:
                r.wait("s0", "s1", "s2")
                r.full[...] = state + r.state[...] + r.s2[...] + r.s1[...] + r.s0[...]
                for x in range(4):
                    for comp in range(2):
                        for q in range(4):
                            at = comp * 8 + q * 2
                            r.sum_o[x, comp, :, q * 512 : (q + 1) * 512] = r.full[at : at + 2, :]
                return
            r.state_o[...] = state
            ham_rows(r, state, r.rows_o)
            ghost_out(r, order)

        return body

    def local_body(order):
        def body(r):
            r.all_points = all_points
            r.wait("pot")
            term = local_term(r, order)
            for comp in range(2):
                r.local_o[comp * 80 : (comp + 1) * 80, :] = term[comp]
            if order == 4:
                r.wait("u0", "u1", "u2")
                r.local_o[...] = r.local_o[...] + r.u0[...] + r.u1[...] + r.u2[...] + r.u[...]

        return body

    def dipole_body(order):
        def body(r):
            r.all_points = all_points
            if order == 4:
                ghost_out(r, order)
            r.wait("ys", "field")
            dipole_image(r)
            term = dipole_term(r, order)
            for comp in range(2):
                at = slice(comp * 80 + 8, comp * 80 + 16)
                r.dip[at, :] = term[comp][8:16, :] + (r.more_o if order == 4 else r.more)[comp]
            for comp in range(2):
                at = comp * 80
                if order == 4:
                    r.psi_o[comp, 0:8, :] = r.local[at + 8 : at + 16, :] + r.dip[at + 8 : at + 16, :]
                    r.psi_o[comp, 8:64, :] = r.local[at + 16 : at + 72, :] + term[comp][16:72, :]
                    r.mark_o[comp] = term[comp][0:8, 0:128]
                else:
                    total = r.local[at : at + 80, :] + term[comp]
                    r.u_o[at : at + 80, :] = total
                    r.u_o[at + 8 : at + 16, :] = r.local[at + 8 : at + 16, :] + r.dip[at + 8 : at + 16, :]
                    r.low_o[at : at + 80, :] = r.u_o[at : at + 80, :].astype(BF16)
            if order < 4:
                first_out(r, r.u_o[8:9, :], r.u_o[88:89, :])
                r.piece[:, 0:512] = r.rows[...]
                z_out(r)

        return body

    for order in range(1, 5):
        zr = over_z(out["zo"])
        ys = lax.all_gather(out["low_o"], "chan", axis=0)
        local_ins = {"info": info, "pot": pot, "u": outer[-1]}
        if order == 4:
            local_ins.update(u0=outer[0], u1=outer[1], u2=outer[2])
        local = call(local_body(order), local_ins, {"local_o": outer_spec}, local_scratch, 1_000_000_000)["local_o"]
        part = call(
            surface_body, {"sym": common["sym"], "after": local, "state": inner[-1], "zr": zr, "amp": amp}, {"po": ((8, 32, 512), BF16)},
            surface_scratch, 1_500_000_000
        )["po"]
        pr = lax.all_to_all(part, "chan", 0, 0)
        inner_ins = {"info": info, "zr": zr, "pr": pr, "state": inner[-1]}
        ghost_ins = {**common, "pr": pr, "amp": amp}
        if order == 4:
            for i in range(3):
                inner_ins["s%d" % i] = inner[i]
        ins = {"info": info, "ys": ys, "dipole": dipole, "field": strength, "local": local}
        more_spec = ((2, 8, 512), F32)
        if order < 4:
            outs = {"state_o": inner_spec, "rows_o": ((1, 512), F32), "more_o": more_spec}
            part = call(
                middle_body(order), {**inner_ins, **ghost_ins, "ham": hams}, outs, {**full_scratch, **z_scratch}, 2_000_000_000
            )
            inner.append(part["state_o"])
            ins.update(more=part["more_o"], rows=part["rows_o"])
            outs = {"zo": z_spec, "u_o": outer_spec, "low_o": low_spec}
            out = call(dipole_body(order), ins, outs, {**dipole_scratch, **z_scratch}, 4_000_000_000)
            outer.append(out["u_o"])
        else:
            total = call(middle_body(4), inner_ins, {"sum_o": ((4, 2, 2, 2048), F32)}, full_scratch, 1_000_000_000)["sum_o"]
            ins.update(ghost_ins)
            outs = {"psi_o": ((2, 64, 512), F32), "mark_o": ((2, 8, 128), F32), "more_o": more_spec}
            out = call(dipole_body(4), ins, outs, dipole_scratch, 4_000_000_000)


    def finish(r):
        r.wait("sums")
        r.state_o[...] = r.sums[0]

    state_next = call(
        finish, {"sums": over_x(total), "mark": out["mark_o"]}, {"state_o": ((2, 2, 2048), F32)}, {}, 1_000_000
    )["state_o"]
    return out["psi_o"].transpose(0, 2, 1), state_next


def solution(mesh):
    return jax.shard_map(
        shards,
        mesh=mesh,
        in_specs=(
            P(None, "chan", "sector"),
            P("chan", "sector"),
            P("chan", None, None, None),
            P("chan", None),
            P("chan", None),
            P("chan"),
            P("chan"),
            P("chan", "sector", None),
            P(None, "chan", None),
            P(),
        ),
        out_specs=(P(None, "chan", "sector"), P(None, "chan", None)),
        check_vma=False,
    )
```
